512 devices in a mesh: pot: 128 (over z_lo, y, x, core), grid: 4 (over z_hi).
Axes of the slice: x: 4, y: 8, z: 8 (z_hi: 4, z_lo: 2; z = z_hi * 2 + z_lo), core: 2. Of those that a mesh axis runs over, the one named last changes fastest.
Arguments:
- potentials: float32 [128, 32, 4096], P('pot', 'grid'), may hold values from -24 to 24
- orbitals: bfloat16 [32, 32, 4096], P(None, 'grid', 'pot'), may hold values from -0.5 to 2
- energies: float32 [32], replicated, may hold values from -2 to -0.2
- local_potential: float32 [32, 4096], replicated, may hold values from 0 to 3
- inverse_factor: bfloat16 [128, 128], replicated, may hold values from -8 to 8, as said below
Outputs:
- updated: float32 [128, 32, 4096], P('pot', 'grid')
- margins: float32 [128, 128], P('pot')
The draws below stay inside these ranges and needn't reach their ends.
Inputs may be any that keep to these rules, and one draw needn't show every extreme that they name: `inverse_factor`: lower triangular with a positive diagonal.
All inputs are finite; a program needn't handle non-finite values.
Results may differ from the reference program's by a relative error of at most 0.0029.
Values may be sent and summed in bfloat16 or wider, within the bound.
A program may use at most 64 MiB of HBM per device.

```python
import jax
import jax.numpy as jnp
from jax import lax

NX = 64
NY = 64
NZ = 32
ORBITALS = 32
SWEEPS = 4
POTENTIALS = 128


def draw_inverse_factor(key, part):
    key_lower, key_diagonal = jax.random.split(jax.random.fold_in(key, 11), 2)
    count_all = POTENTIALS
    strict_lower = jnp.tril(jax.random.normal(key_lower, (count_all, count_all), jnp.float32) * 0.5 / jnp.sqrt(1.0 * count_all), -1)
    diagonal = jnp.exp(jax.random.uniform(key_diagonal, (count_all,), jnp.float32, jnp.log(0.5), jnp.log(2.0)))
    matrix = strict_lower + jnp.diag(diagonal)
    return matrix.astype(jnp.bfloat16)


def raised(array, key, source, target, shards_of, factor):
    def block_of(dim):
        return (jnp.arange(array.shape[dim]) // (array.shape[dim] // shards_of)).reshape((-1,) + (1,) * (array.ndim - 1 - dim))

    near = jax.random.permutation(key, shards_of)[block_of(target)]
    far = (block_of(target) + shards_of // 2) % shards_of
    return jnp.where((block_of(source) == near) | (block_of(source) == far), factor * array, array)


def steps_of(rng, extent, cuts, least, largest):
    gain = 1.0
    for position, shards_of in cuts:
        draws = jax.random.uniform(jax.random.fold_in(jax.random.fold_in(rng, 6), position), (shards_of,), jnp.float32, least / len(cuts), largest / len(cuts))
        gain = gain * jnp.repeat(jnp.exp(draws), extent[position] // shards_of).reshape((-1,) + (1,) * (len(extent) - 1 - position))
    return gain


def noise_with(stream_key, shape, spread, most, pieces, heavy, kind=jnp.bfloat16):
    array = spread * jax.random.normal(stream_key, shape, jnp.float32)
    if pieces:
        array = array * steps_of(stream_key, shape, pieces, -0.22, 0.18)
    return jnp.clip(raised(array, jax.random.fold_in(stream_key, 3), *heavy), -most, most).astype(kind)


def setup_inputs(seed: int = 0) -> dict:
    streams_of = jax.random.split(jax.random.key(seed), 6)
    return {
        "potentials": noise_with(streams_of[0], (POTENTIALS, NZ, NX * NY), 1.0, 24.0, ((0, 128), (1, 4)), (2, 0, 128, 5.5), jnp.float32),
        "orbitals": jnp.clip(-0.5 + 2.5 * jax.random.uniform(streams_of[1], (ORBITALS, NZ, NX * NY), jnp.float32) ** steps_of(streams_of[1], (ORBITALS, NZ, NX * NY), ((1, 4), (2, 128)), -0.2, 0.2), -0.5, 2.0).astype(jnp.bfloat16),
        "energies": jnp.clip(jax.random.uniform(streams_of[2], (ORBITALS,), jnp.float32, -2.0, -0.2), -2.0, -0.2),
        "local_potential": jnp.clip(jax.random.uniform(streams_of[3], (NZ, NX * NY), jnp.float32, 0.0, 3.0), 0.0, 3.0),
        "inverse_factor": draw_inverse_factor(jax.random.fold_in(streams_of[5], 71), 0),
    }


DAMPING = 0.8


def plane_neighbours(field, row_width):
    plane_size = field.shape[-1]
    widths = [(0, 0)] * (field.ndim - 1)
    padded = jnp.pad(field, widths + [(row_width, row_width)])
    along_y = padded[..., 2 * row_width:] + padded[..., :plane_size]
    column = jnp.arange(plane_size, dtype=jnp.int32) % row_width
    padded = jnp.pad(field, widths + [(1, 1)])
    right_side = jnp.where(column == row_width - 1, 0.0, padded[..., 2:])
    left_side = jnp.where(column == 0, 0.0, padded[..., :plane_size])
    return along_y + right_side + left_side


def plane_pairs(field):
    padded = jnp.pad(field, [(0, 0)] * (field.ndim - 2) + [(1, 1), (0, 0)])
    return padded[..., 2:, :] + padded[..., :-2, :]


def reference(potentials, orbitals, energies, local_potential, inverse_factor):
    def per_orbital(summed, member):
        orbital, energy = member
        orbital = orbital.astype(jnp.float32)
        diagonal = 3.0 + local_potential - energy
        source = -orbital * potentials
        answer = DAMPING * source / diagonal
        for sweep_index in range(SWEEPS - 1):
            nearby = plane_pairs(answer) + plane_neighbours(answer, NX)
            answer = answer + DAMPING * (source - diagonal * answer + 0.5 * nearby) / diagonal
        return summed + orbital * answer, None

    summed, _ = lax.scan(per_orbital, jnp.zeros_like(potentials), (orbitals, energies))
    trial_block = (potentials + (4.0 / ORBITALS) * summed).astype(jnp.bfloat16)
    flattened = trial_block.reshape(trial_block.shape[0], -1)
    margins = lax.dot_general(flattened, flattened, (((1,), (1,)), ((), ())), preferred_element_type=jnp.float32)
    margins = margins / (NX * NY * NZ)
    updated = jnp.dot(inverse_factor, flattened, preferred_element_type=jnp.float32).reshape(trial_block.shape)
    return updated, margins
```

```python
import functools

import jax
import jax.numpy as jnp
from jax import lax
from jax.experimental import pallas as pl
from jax.experimental.pallas import tpu as pltpu
from jax.sharding import PartitionSpec as P

MESH = pl.DeviceIdType.MESH
F32 = jnp.float32
BF16 = jnp.bfloat16
NZ = 32
NPAIR = 32
ROWS2D = [(dz, dy) for dz in range(-3, 4) for dy in range(-3, 4) if abs(dz) + abs(dy) <= 3]
INDEX2D = {pair: number for number, pair in enumerate(ROWS2D)}
OFFSETS = [
    (dz, dy, dx)
    for dz, dy in ROWS2D
    for dx in range(-3, 4)
    if abs(dz) + abs(dy) + abs(dx) <= 3
]
COUNT = len(OFFSETS)
LINES = sorted({(3 + zl + dz, 3 + yl + dy) for dz, dy in ROWS2D for zl in range(2) for yl in range(2)})
FAR = 1e30


def tile_of(p):
    core, x, y, low = p % 2, (p // 2) % 4, (p // 8) % 8, p // 64
    return low * 2 + core, y * 4 + x + (y % 2) * (3 - 2 * x)


def device_of(zp, yt):
    y, s = yt // 4, yt % 4
    return (zp // 2) * 64 + y * 8 + (s + (y % 2) * (3 - 2 * s)) * 2 + zp % 2


def place(zt, yt):
    return device_of(zt % 4, yt), zt // 4


def build_fields(zt, yt, loc, erow, orbs, pads, ls, bl, wf, pf):
    for m in range(5):
        pp = yt - 2 + m
        ok = jnp.logical_and(pp >= 0, pp < NPAIR)
        pc = jnp.clip(pp, 0, NPAIR - 1)
        column = loc[:, pl.ds(pl.multiple_of(pc * 128, 128), 128)]
        pads[m, 0:8, :] = jnp.full((8, 128), FAR, F32)
        pads[m, 40:48, :] = jnp.full((8, 128), FAR, F32)
        pads[m, 8:40, :] = jnp.where(ok, column, FAR)
        ls[m * 8 : m * 8 + 8, :] = pads[m, pl.ds(2 * zt + 5, 8), :]
    lt = ls[...].T
    for number, (k, r) in enumerate(LINES):
        m, yl = (r + 1) // 2, (r + 1) % 2
        c = m * 8 + k
        bl[number] = jnp.broadcast_to(lt[yl * 64 : yl * 64 + 64, c : c + 1], (64, 128))
    group = lax.broadcasted_iota(jnp.int32, (64, 128), 1) // 32
    group16 = lax.broadcasted_iota(jnp.int32, (16, 128), 1) // 32
    line_index = {line: number for number, line in enumerate(LINES)}
    shift3 = 3.0 - erow[...]
    zeros = jnp.zeros((8, 128), F32)
    for number, (dz, dy) in enumerate(ROWS2D):
        at = None
        lines = [(3 + zl + dz, 3 + yl + dy) for zl in range(2) for yl in range(2)]
        for l, line in enumerate(lines):
            here = bl[line_index[line]]
            at = here if at is None else jnp.where(group == l, here, at)
        w = jnp.where(at > 0.1 * FAR, 0.0, 0.4 / (at + shift3))
        wf[number, 0:8, :] = zeros
        wf[number, 72:80, :] = zeros
        wf[number, 8:72, :] = w
        pf[number, 0:8, :] = zeros
        pf[number, 72:80, :] = zeros
        for h in range(2):
            for xq in range(2):
                orb = None
                for l, (k, r) in enumerate(lines):
                    q, zl = (k + 1) // 2, (k + 1) % 2
                    unit = orbs[r, h, q].astype(F32)
                    shift = (l * 32 - zl * 64 - xq * 32) % 128
                    if shift:
                        unit = pltpu.roll(unit, shift, 1)
                    orb = unit if orb is None else jnp.where(group16 == l, unit, orb)
                x0 = h * 32 + xq * 16
                pf[number, 8 + x0 : 24 + x0, :] = orb * w[x0 : x0 + 16]


def build_products(wf, pf, sf, qb):
    def w(dz, dy, dx):
        return wf[INDEX2D[(dz, dy)], 8 + dx : 72 + dx, :]

    cross = [(0, 0), (1, 0), (-1, 0), (0, 1), (0, -1)]
    for number, (dz, dy) in enumerate(cross):
        i = INDEX2D[(dz, dy)]
        total = wf[i, 3:75, :] + wf[i, 5:77, :]
        for ez, ey in cross[1:]:
            total = total + wf[INDEX2D[(dz + ez, dy + ey)], 4:76, :]
        sf[number, 4:76, :] = total

    def s1(dz, dy, dx):
        return sf[cross.index((dz, dy)), 8 + dx : 72 + dx, :]

    def unit(axis, sign):
        return tuple(sign if a == axis else 0 for a in range(3))

    def plus(a, b):
        return tuple(x + y for x, y in zip(a, b))

    mine = -0.25 * pf[INDEX2D[(0, 0)], 8:72, :]
    for number, offset in enumerate(OFFSETS):
        dist = sum(abs(c) for c in offset)
        steps = []
        for axis in range(3):
            if offset[axis]:
                steps.append((unit(axis, 1 if offset[axis] > 0 else -1), abs(offset[axis])))
        if dist == 0:
            orb = 1.248 / w(0, 0, 0)
            path = orb + 1.6 * s1(0, 0, 0)
        elif dist == 1:
            e = offset
            w0, we = w(0, 0, 0), w(*e)
            path = 1.52 + w0 * (s1(0, 0, 0) - we) + we * s1(*e)
            for axis in range(3):
                if not e[axis]:
                    for sign in (1, -1):
                        b = unit(axis, sign)
                        path = path + w(*b) * w(*plus(b, e))
        elif dist == 2:
            if len(steps) == 1:
                path = 1.6 * w(*steps[0][0])
            else:
                path = 1.6 * (w(*steps[0][0]) + w(*steps[1][0]))
        elif len(steps) == 1:
            a = steps[0][0]
            path = w(*a) * w(*plus(a, a))
        elif len(steps) == 2:
            (a, b) = (steps[0][0], steps[1][0]) if steps[0][1] == 2 else (steps[1][0], steps[0][0])
            ab = w(*plus(a, b))
            path = w(*a) * (w(*plus(a, a)) + ab) + w(*b) * ab
        else:
            a, b, c = (s[0] for s in steps)
            ab, ac, bc = w(*plus(a, b)), w(*plus(a, c)), w(*plus(b, c))
            path = w(*a) * (ab + ac) + w(*b) * (ab + bc) + w(*c) * (ac + bc)
        dz, dy, dx = offset
        q = mine * pf[INDEX2D[(dz, dy)], 8 + dx : 72 + dx, :] * path
        high = q.astype(BF16)
        qb[number * 64 : number * 64 + 64, 0:128] = high
        qb[number * 64 : number * 64 + 64, 128:256] = (q - high.astype(F32)).astype(BF16)


def build_coefficients(qb, coef):
    k = lax.broadcasted_iota(jnp.int32, (256, 512), 0)
    n = lax.broadcasted_iota(jnp.int32, (256, 512), 1)
    spread = jnp.where((k % 128) // 32 == n // 128, 1.0, 0.0).astype(BF16)

    @pl.loop(0, 9)
    def _(step):
        rows = pl.ds(pl.multiple_of(step * 448, 448), 448)
        coef[rows, :] = jnp.dot(qb[rows, :], spread, preferred_element_type=F32)


def apply_stencil(own, halo, vf, coef):
    zeros = jnp.zeros((8, 128), F32)
    for number, (k, r) in enumerate(LINES):
        vf[number, 0:8, :] = zeros
        vf[number, 72:80, :] = zeros
        if 3 <= k <= 4 and 3 <= r <= 4:
            vf[number, 8:72, :] = own[k - 3, r - 3]
        else:
            vf[number, 8:72, :] = halo[k, r].astype(F32)
    line_index = {line: number for number, line in enumerate(LINES)}
    trial = []
    for l in range(4):
        zl, yl = l // 2, l % 2
        total = own[zl, yl]
        for number, (dz, dy, dx) in enumerate(OFFSETS):
            field = vf[line_index[(3 + zl + dz, 3 + yl + dy)], 8 + dx : 72 + dx, :]
            total = total + coef[number * 64 : number * 64 + 64, l * 128 : l * 128 + 128] * field
        trial.append(total)
    return trial


def finish(trial, factor, ug):
    columns = []
    for zl in range(2):
        plane = jnp.concatenate([trial[2 * zl], trial[2 * zl + 1]], axis=0)
        columns.append(plane.T.astype(BF16))
    gram = None
    for zl in range(2):
        ug[zl] = jnp.dot(factor[...], columns[zl], preferred_element_type=F32)
        part = lax.dot_general(columns[zl], columns[zl], (((1,), (1,)), ((), ())), preferred_element_type=F32)
        gram = part if gram is None else gram + part
    ug[2] = gram * (1.0 / 131072.0)


def local_kernel(coords, own, halo, orbs, loc, erow, factor, ug, pads, ls, bl, wf, pf, sf, qb, coef, vf):
    zt, yt = coords()
    build_fields(zt, yt, loc, erow, orbs, pads, ls, bl, wf, pf)
    build_products(wf, pf, sf, qb)
    build_coefficients(qb, coef)
    finish(apply_stencil(own, halo, vf, coef), factor, ug)


LOCAL_SCRATCH = [
    pltpu.VMEM((5, 48, 128), F32),
    pltpu.VMEM((128, 128), F32),
    pltpu.VMEM((len(LINES), 64, 128), F32),
    pltpu.VMEM((len(ROWS2D), 80, 128), F32),
    pltpu.VMEM((len(ROWS2D), 80, 128), F32),
    pltpu.VMEM((5, 80, 128), F32),
    pltpu.VMEM((COUNT * 64, 256), BF16),
    pltpu.VMEM((COUNT * 64, 512), F32),
    pltpu.VMEM((len(LINES), 80, 128), F32),
]


def local_part(coords, own, halo, orbs, loc, erow, factor):
    vmem = pl.BlockSpec(memory_space=pltpu.VMEM)
    return pl.pallas_call(
        functools.partial(local_kernel, coords),
        out_shape=jax.ShapeDtypeStruct((3, 128, 128), F32),
        in_specs=[vmem] * 6,
        out_specs=vmem,
        scratch_shapes=LOCAL_SCRATCH,
        compiler_params=pltpu.CompilerParams(vmem_limit_bytes=48 * 1024 * 1024),
    )(own, halo, orbs, loc, erow, factor)


NEIGHBOURS = [
    (1, 0, 0, 2, 0, 2), (-1, 0, 0, 2, 0, 2), (0, 1, 0, 2, 0, 2), (0, -1, 0, 2, 0, 2),
    (2, 0, 1, 1, 0, 2), (-2, 0, 0, 1, 0, 2), (0, 2, 0, 2, 1, 1), (0, -2, 0, 2, 0, 1),
    (1, 1, 1, 1, 0, 2), (1, -1, 1, 1, 0, 2), (-1, 1, 0, 1, 0, 2), (-1, -1, 0, 1, 0, 2),
    (1, 1, 0, 1, 1, 1), (1, -1, 0, 1, 0, 1), (-1, 1, 1, 1, 1, 1), (-1, -1, 1, 1, 0, 1),
]
PEERS = sorted({(a, b) for a, b, *_ in NEIGHBOURS})


def coords_here():
    zp, yt = tile_of(lax.axis_index("pot"))
    return lax.axis_index("grid") * 4 + zp, yt


def inward_kernel(rows_in, orb_in, own, halo, orbs, recv, lines, packed,
                  row_send, row_recv, slab_send, slab_recv, orb_send, orb_recv, halo_send, halo_recv):
    me, g = lax.axis_index("pot"), lax.axis_index("grid")
    zp, yt = tile_of(me)
    zt = g * 4 + zp
    up, down = (g + 1) % 4, (g + 3) % 4

    barrier = pltpu.get_barrier_semaphore()

    @pl.loop(1, 128)
    def _(step):
        pl.semaphore_signal(barrier, inc=1, device_id=((me + step) % 128, g), device_id_type=MESH)

    for other in (up, down):
        pl.semaphore_signal(barrier, inc=1, device_id=(me, other), device_id_type=MESH)
    for a, b in PEERS:
        peer = place((zt + a) % 16, (yt + b) % 32)
        pl.semaphore_signal(barrier, inc=1, device_id=peer, device_id_type=MESH)
    pl.semaphore_wait(barrier, 127 + 2 + len(PEERS))

    to_up = pltpu.make_async_remote_copy(
        orb_in.at[2:4], packed.at[0:2], slab_send.at[0], slab_recv.at[0], device_id=(me, up), device_id_type=MESH)
    to_down = pltpu.make_async_remote_copy(
        orb_in.at[0:2], packed.at[6:8], slab_send.at[1], slab_recv.at[1], device_id=(me, down), device_id_type=MESH)
    to_up.start()
    to_down.start()
    packed[2:6] = orb_in[...]

    @pl.loop(1, 128)
    def _(step):
        to = (me + step) % 128
        to_zp, to_yt = tile_of(to)
        pltpu.make_async_remote_copy(
            rows_in.at[:, to_zp * 32 + to_yt, :], recv.at[:, me, :], row_send, row_recv,
            device_id=(to, g), device_id_type=MESH).start()

    keep = pltpu.make_async_copy(rows_in.at[:, zp * 32 + yt, :], recv.at[:, me, :], row_recv)
    keep.start()
    to_up.wait()
    to_down.wait()

    row, half = me // 2, me % 2
    odd = row % 2
    for m in range(4):
        rr = 2 * m + 1 - odd
        to_yt = ((row + 3 - rr + 32 * 2) // 2) % 32
        for to_zp in range(4):
            to = device_of(to_zp, to_yt)
            source, target = packed.at[to_zp : to_zp + 5], orbs.at[rr, half]

            @pl.when(to != me)
            def _():
                pltpu.make_async_remote_copy(
                    source, target, orb_send, orb_recv, device_id=(to, g), device_id_type=MESH).start()

            @pl.when(to == me)
            def _():
                pltpu.make_async_copy(source, target, orb_recv).start()

    pltpu.make_async_copy(recv, recv, row_recv).wait()
    for zl in range(2):
        plane = recv[zl].T
        for yl in range(2):
            line = plane[yl * 64 : yl * 64 + 64]
            own[zl, yl] = line
            lines[zl, yl] = line.astype(BF16)
    copies = []
    for number, (a, b, z0, nz, y0, ny) in enumerate(NEIGHBOURS):
        peer = place((zt + a) % 16, (yt + b) % 32)
        zz, yy = 3 - 2 * a + z0, 3 - 2 * b + y0
        copies.append(pltpu.make_async_remote_copy(
            lines.at[z0 : z0 + nz, y0 : y0 + ny], halo.at[zz : zz + nz, yy : yy + ny],
            halo_send.at[number], halo_recv.at[number], device_id=peer, device_id_type=MESH))
        copies[-1].start()
    pltpu.make_async_copy(orbs, orbs, orb_recv).wait()
    for copy in copies:
        copy.wait()
    pltpu.make_async_copy(rows_in.at[:, 0:127, :], rows_in.at[:, 0:127, :], row_send).wait()

    count = 16
    same = 0
    for m in range(4):
        rr = 2 * m + 1 - odd
        to_yt = ((row + 3 - rr + 32 * 2) // 2) % 32
        for to_zp in range(4):
            same = same + jnp.where(device_of(to_zp, to_yt) == me, 1, 0)

    @pl.when(same == 0)
    def _():
        pltpu.make_async_copy(orbs, orbs, orb_send).wait()

    @pl.when(same != 0)
    def _():
        flat = orbs.at[0:7]
        pltpu.make_async_copy(flat, flat, orb_send).wait()
        pltpu.make_async_copy(orbs.at[7, 0], orbs.at[7, 0], orb_send).wait()


def inward(rows_in, orb_in):
    vmem = pl.BlockSpec(memory_space=pltpu.VMEM)
    return pl.pallas_call(
        inward_kernel,
        out_shape=(
            jax.ShapeDtypeStruct((2, 2, 64, 128), F32),
            jax.ShapeDtypeStruct((8, 8, 64, 128), BF16),
            jax.ShapeDtypeStruct((8, 2, 5, 16, 128), BF16),
        ),
        in_specs=[vmem] * 2,
        out_specs=(vmem,) * 3,
        scratch_shapes=[
            pltpu.VMEM((2, 128, 128), F32),
            pltpu.VMEM((2, 2, 64, 128), BF16),
            pltpu.VMEM((8, 16, 128), BF16),
            pltpu.SemaphoreType.DMA, pltpu.SemaphoreType.DMA,
            pltpu.SemaphoreType.DMA((2,)), pltpu.SemaphoreType.DMA((2,)),
            pltpu.SemaphoreType.DMA, pltpu.SemaphoreType.DMA,
            pltpu.SemaphoreType.DMA((16,)), pltpu.SemaphoreType.DMA((16,)),
        ],
        compiler_params=pltpu.CompilerParams(
            collective_id=0, has_side_effects=True, vmem_limit_bytes=32 * 1024 * 1024),
    )(rows_in, orb_in)


def outward_kernel(ug, out, margins, back, parts, send, recv, part_send, part_recv):
    me, g = lax.axis_index("pot"), lax.axis_index("grid")
    zp, yt = tile_of(me)
    slot = zp * 32 + yt
    barrier = pltpu.get_barrier_semaphore()

    @pl.loop(1, 128)
    def _(step):
        pl.semaphore_signal(barrier, inc=1, device_id=((me + step) % 128, g), device_id_type=MESH)

    for step in range(1, 4):
        pl.semaphore_signal(barrier, inc=1, device_id=(me, (g + step) % 4), device_id_type=MESH)
    pl.semaphore_wait(barrier, 130)

    @pl.loop(1, 128)
    def _(step):
        to = (me + step) % 128
        pltpu.make_async_remote_copy(
            ug.at[:, to, :], back.at[:, slot, :], send, recv, device_id=(to, g), device_id_type=MESH).start()

    pltpu.make_async_copy(ug.at[:, me, :], back.at[:, slot, :], recv).start()
    pltpu.make_async_copy(back, back, recv).wait()
    parts[0] = jnp.broadcast_to(jnp.sum(back[2], axis=0, keepdims=True), (8, 128))
    copies = []
    for step in range(1, 4):
        copies.append(pltpu.make_async_remote_copy(
            parts.at[0], parts.at[4 - step], part_send.at[step - 1], part_recv.at[step - 1],
            device_id=(me, (g + step) % 4), device_id_type=MESH))
        copies[-1].start()
    for z in range(8):
        rows = back[z % 2, (z // 2) * 32 : (z // 2) * 32 + 32, :]
        for y in range(32):
            out[0, z : z + 1, y * 128 : y * 128 + 128] = rows[y : y + 1]
    for copy in copies:
        copy.wait()
    total = None
    for slab in range(4):
        part = parts[(slab - g + 4) % 4]
        total = part if total is None else total + part
    margins[...] = total[0:1]
    pltpu.make_async_copy(ug.at[:, 0:127, :], ug.at[:, 0:127, :], send).wait()


def outward(ug):
    vmem = pl.BlockSpec(memory_space=pltpu.VMEM)
    return pl.pallas_call(
        outward_kernel,
        out_shape=(jax.ShapeDtypeStruct((1, 8, 4096), F32), jax.ShapeDtypeStruct((1, 128), F32)),
        in_specs=[vmem],
        out_specs=(vmem,) * 2,
        scratch_shapes=[
            pltpu.VMEM((3, 128, 128), F32),
            pltpu.VMEM((4, 8, 128), F32),
            pltpu.SemaphoreType.DMA, pltpu.SemaphoreType.DMA,
            pltpu.SemaphoreType.DMA((3,)), pltpu.SemaphoreType.DMA((3,)),
        ],
        compiler_params=pltpu.CompilerParams(
            collective_id=1, has_side_effects=True, vmem_limit_bytes=32 * 1024 * 1024),
    )(ug)


def prepared(potentials, orbitals, energies):
    rows = potentials.reshape(4, 2, 32, 128).transpose(1, 0, 2, 3).reshape(2, 128, 128)
    packed = orbitals.reshape(32, 4, 2, 2, 16).transpose(1, 4, 2, 3, 0).reshape(4, 16, 128)
    return rows, packed, jnp.tile(energies, 4).reshape(1, 128)


def local(potentials, orbitals, energies, local_potential, inverse_factor):
    rows, packed, erow = prepared(potentials, orbitals, energies)
    own, halo, orbs = inward(rows, packed)
    ug = local_part(coords_here, own, halo, orbs, local_potential, erow, inverse_factor)
    return outward(ug)


def solution(mesh):
    in_specs = (P("pot", "grid", None), P(None, "grid", "pot"), P(), P(), P())
    out_specs = (P("pot", "grid", None), P("pot", None))
    return jax.shard_map(local, mesh=mesh, in_specs=in_specs, out_specs=out_specs, check_vma=False)
```

```python
import jax
import jax.numpy as jnp
from jax import lax
from jax.experimental import pallas as pl
from jax.experimental.pallas import tpu as pltpu
from jax.sharding import PartitionSpec as P

MESH = pl.DeviceIdType.MESH
F32 = jnp.float32
BF16 = jnp.bfloat16
NZ = 32
NPAIR = 32
ROWS2D = [(dz, dy) for dz in range(-3, 4) for dy in range(-3, 4) if abs(dz) + abs(dy) <= 3]
INDEX2D = {pair: number for number, pair in enumerate(ROWS2D)}
OFFSETS = [
    (dz, dy, dx)
    for dz, dy in ROWS2D
    for dx in range(-3, 4)
    if abs(dz) + abs(dy) + abs(dx) <= 3
]
COUNT = len(OFFSETS)
LINES = sorted({(3 + zl + dz, 3 + yl + dy) for dz, dy in ROWS2D for zl in range(2) for yl in range(2)})
LINE_INDEX = {line: number for number, line in enumerate(LINES)}
CROSS = [(0, 0), (1, 0), (-1, 0), (0, 1), (0, -1)]
FAR = 1e30


def tile_of(p):
    core, x, y, low = p % 2, (p // 2) % 4, (p // 8) % 8, p // 64
    return low * 2 + core, y * 4 + x + (y % 2) * (3 - 2 * x)


def device_of(zp, yt):
    y, s = yt // 4, yt % 4
    return (zp // 2) * 64 + y * 8 + (s + (y % 2) * (3 - 2 * s)) * 2 + zp % 2


def place(zt, yt):
    return device_of(zt % 4, yt), zt // 4


def line_sets(dz, dy):
    return [(3 + zl + dz, 3 + yl + dy) for zl in range(2) for yl in range(2)]


def build_weights(zt, yt, loc, energies, pads, ls, bl, wf, sf):
    for m in range(5):
        pp = yt - 2 + m
        ok = jnp.logical_and(pp >= 0, pp < NPAIR)
        pc = jnp.clip(pp, 0, NPAIR - 1)
        column = loc[:, pl.ds(pl.multiple_of(pc * 128, 128), 128)]
        pads[m, 0:8, :] = jnp.full((8, 128), FAR, F32)
        pads[m, 40:48, :] = jnp.full((8, 128), FAR, F32)
        pads[m, 8:40, :] = jnp.where(ok, column, FAR)
        ls[m * 8 : m * 8 + 8, :] = pads[m, pl.ds(2 * zt + 5, 8), :]
    lt = ls[...].T
    for number, (k, r) in enumerate(LINES):
        m, yl = (r + 1) // 2, (r + 1) % 2
        c = m * 8 + k
        bl[number] = jnp.broadcast_to(lt[yl * 64 : yl * 64 + 64, c : c + 1], (64, 128))
    group = lax.broadcasted_iota(jnp.int32, (64, 128), 1) // 32
    row = energies[...]
    shift3 = 3.0 - jnp.concatenate([row, row, row, row], axis=1)
    zeros = jnp.zeros((8, 128), F32)
    for number, (dz, dy) in enumerate(ROWS2D):
        at = None
        for l, line in enumerate(line_sets(dz, dy)):
            here = bl[LINE_INDEX[line]]
            at = here if at is None else jnp.where(group == l, here, at)
        wf[number, 0:8, :] = zeros
        wf[number, 72:80, :] = zeros
        wf[number, 8:72, :] = jnp.where(at > 0.1 * FAR, 0.0, 0.4 / (at + shift3))
    for number, (dz, dy) in enumerate(CROSS):
        i = INDEX2D[(dz, dy)]
        total = wf[i, 3:75, :] + wf[i, 5:77, :]
        for ez, ey in CROSS[1:]:
            total = total + wf[INDEX2D[(dz + ez, dy + ey)], 4:76, :]
        sf[number, 4:76, :] = total


def build_orbitals(orbs, wf, pf):
    group = lax.broadcasted_iota(jnp.int32, (16, 128), 1) // 32
    zeros = jnp.zeros((8, 128), F32)
    for number, (dz, dy) in enumerate(ROWS2D):
        pf[number, 0:8, :] = zeros
        pf[number, 72:80, :] = zeros
        for h in range(2):
            for xq in range(2):
                orb = None
                for l, (k, r) in enumerate(line_sets(dz, dy)):
                    q, zl = (k + 1) // 2, (k + 1) % 2
                    unit = orbs[q, r, h].astype(F32)
                    shift = (l * 32 - zl * 64 - xq * 32) % 128
                    if shift:
                        unit = pltpu.roll(unit, shift, 1)
                    orb = unit if orb is None else jnp.where(group == l, unit, orb)
                x0 = 8 + h * 32 + xq * 16
                pf[number, x0 : x0 + 16, :] = orb * wf[number, x0 : x0 + 16, :]


def build_products(wf, pf, sf, qb):
    def w(dz, dy, dx):
        return wf[INDEX2D[(dz, dy)], 8 + dx : 72 + dx, :]

    def s1(dz, dy, dx):
        return sf[CROSS.index((dz, dy)), 8 + dx : 72 + dx, :]

    def unit(axis, sign):
        return tuple(sign if a == axis else 0 for a in range(3))

    def plus(a, b):
        return tuple(x + y for x, y in zip(a, b))

    mine = -0.25 * pf[INDEX2D[(0, 0)], 8:72, :]
    for number, offset in enumerate(OFFSETS):
        dist = sum(abs(c) for c in offset)
        steps = []
        for axis in range(3):
            if offset[axis]:
                steps.append((unit(axis, 1 if offset[axis] > 0 else -1), abs(offset[axis])))
        if dist == 0:
            orb = 1.248 / w(0, 0, 0)
            path = orb + 1.6 * s1(0, 0, 0)
        elif dist == 1:
            e = offset
            w0, we = w(0, 0, 0), w(*e)
            path = 1.52 + w0 * (s1(0, 0, 0) - we) + we * s1(*e)
            for axis in range(3):
                if not e[axis]:
                    for sign in (1, -1):
                        b = unit(axis, sign)
                        path = path + w(*b) * w(*plus(b, e))
        elif dist == 2:
            if len(steps) == 1:
                path = 1.6 * w(*steps[0][0])
            else:
                path = 1.6 * (w(*steps[0][0]) + w(*steps[1][0]))
        elif len(steps) == 1:
            a = steps[0][0]
            path = w(*a) * w(*plus(a, a))
        elif len(steps) == 2:
            (a, b) = (steps[0][0], steps[1][0]) if steps[0][1] == 2 else (steps[1][0], steps[0][0])
            ab = w(*plus(a, b))
            path = w(*a) * (w(*plus(a, a)) + ab) + w(*b) * ab
        else:
            a, b, c = (s[0] for s in steps)
            ab, ac, bc = w(*plus(a, b)), w(*plus(a, c)), w(*plus(b, c))
            path = w(*a) * (ab + ac) + w(*b) * (ab + bc) + w(*c) * (ac + bc)
        dz, dy, dx = offset
        q = mine * pf[INDEX2D[(dz, dy)], 8 + dx : 72 + dx, :] * path
        high = q.astype(BF16)
        qb[number * 64 : number * 64 + 64, 0:128] = high
        qb[number * 64 : number * 64 + 64, 128:256] = (q - high.astype(F32)).astype(BF16)


def build_coefficients(qb, coef):
    k = lax.broadcasted_iota(jnp.int32, (256, 512), 0)
    n = lax.broadcasted_iota(jnp.int32, (256, 512), 1)
    spread = jnp.where((k % 128) // 32 == n // 128, 1.0, 0.0).astype(BF16)

    @pl.loop(0, 9)
    def _(step):
        rows = pl.ds(pl.multiple_of(step * 448, 448), 448)
        coef[rows, :] = jnp.dot(qb[rows, :], spread, preferred_element_type=F32)


def place_lines(source, inside, vf):
    zeros = jnp.zeros((8, 128), F32)
    for number, (k, r) in enumerate(LINES):
        here = 3 <= k <= 4 and 3 <= r <= 4
        if here != inside:
            continue
        vf[number, 0:8, :] = zeros
        vf[number, 72:80, :] = zeros
        vf[number, 8:72, :] = source[k - 3, r - 3] if here else source[k, r].astype(F32)


def apply_stencil(vf, coef):
    trial = []
    for l in range(4):
        zl, yl = l // 2, l % 2
        total = vf[LINE_INDEX[(3 + zl, 3 + yl)], 8:72, :]
        for number, (dz, dy, dx) in enumerate(OFFSETS):
            field = vf[LINE_INDEX[(3 + zl + dz, 3 + yl + dy)], 8 + dx : 72 + dx, :]
            total = total + coef[number * 64 : number * 64 + 64, l * 128 : l * 128 + 128] * field
        trial.append(total)
    return trial


def finish(trial, factor, ug):
    columns = []
    for zl in range(2):
        plane = jnp.concatenate([trial[2 * zl], trial[2 * zl + 1]], axis=0)
        columns.append(plane.T.astype(BF16))
    gram = None
    for zl in range(2):
        ug[zl] = jnp.dot(factor[...], columns[zl], preferred_element_type=F32)
        part = lax.dot_general(columns[zl], columns[zl], (((1,), (1,)), ((), ())), preferred_element_type=F32)
        gram = part if gram is None else gram + part
    ug[2] = gram * (1.0 / 131072.0)


NEIGHBOURS = [
    (1, 0, 0, 2, 0, 2), (-1, 0, 0, 2, 0, 2), (0, 1, 0, 2, 0, 2), (0, -1, 0, 2, 0, 2),
    (2, 0, 1, 1, 0, 2), (-2, 0, 0, 1, 0, 2), (0, 2, 0, 2, 1, 1), (0, -2, 0, 2, 0, 1),
    (1, 1, 1, 1, 0, 2), (1, -1, 1, 1, 0, 2), (-1, 1, 0, 1, 0, 2), (-1, -1, 0, 1, 0, 2),
    (1, 1, 0, 1, 1, 1), (1, -1, 0, 1, 0, 1), (-1, 1, 1, 1, 1, 1), (-1, -1, 1, 1, 0, 1),
]
ORB_NEIGHBOURS = [
    (1, 0, 0, 2), (-1, 0, 0, 2), (0, 1, 0, 2), (0, -1, 0, 2), (2, 0, 0, 2), (-2, 0, 0, 2),
    (1, 1, 0, 2), (1, -1, 0, 2), (-1, 1, 0, 2), (-1, -1, 0, 2), (0, 2, 1, 1), (0, -2, 0, 1),
]


def ring(distance, size):
    return min(distance, size - distance)


OTHERS = sorted(
    ((y, x, z, c) for y in range(8) for x in range(4) for z in range(2) for c in range(2) if y or x or z or c),
    key=lambda d: (-(ring(d[0], 8) + ring(d[1], 4) + d[2]), d),
)


def kernel(pot, orb_in, energies, loc, factor, out, margins,
           rows_in, recv, lines, own, halo, orbs, ug, back, parts, pads, ls, bl, wf, pf, sf, qb, coef, vf,
           row_send, row_recv, move_send, move_recv, orb_send, orb_recv, halo_send, halo_recv,
           back_send, back_recv, part_send, part_recv):
    me, g = lax.axis_index("pot"), lax.axis_index("grid")
    zp, yt = tile_of(me)
    zt = g * 4 + zp
    ys = [(me // 8 + d) % 8 * 8 for d in range(8)]
    xs = [(me // 2 + d) % 4 * 2 for d in range(4)]
    zs = [me // 64 * 64, (1 - me // 64) * 64]
    cs = [me % 2, 1 - me % 2]

    def others():
        for y, x, z, c in OTHERS:
            yield ys[y] + xs[x] + zs[z] + cs[c]

    def near(a, b):
        return place((zt + a + 16) % 16, (yt + b + 32) % 32)

    barrier = pltpu.get_barrier_semaphore()
    for to in others():
        pl.semaphore_signal(barrier, inc=1, device_id=(to, g), device_id_type=MESH)
    for step in range(1, 4):
        pl.semaphore_signal(barrier, inc=1, device_id=(me, (g + step) % 4), device_id_type=MESH)
    for a, b, *_ in ORB_NEIGHBOURS:
        pl.semaphore_signal(barrier, inc=1, device_id=near(a, b), device_id_type=MESH)

    for z in range(8):
        for y in range(32):
            to = device_of(z // 2, y)
            rows_in[z % 2, to : to + 1, :] = pot[0, z : z + 1, y * 128 : y * 128 + 128]
    build_weights(zt, yt, loc, energies, pads, ls, bl, wf, sf)
    pl.semaphore_wait(barrier, len(OTHERS) + 3 + len(ORB_NEIGHBOURS))

    row, half = me // 2, me % 2
    low, landing = row % 2, (row % 2) * 2 + half
    moves = []
    for to_zp in range(4):
        to = device_of(to_zp, row // 2)
        target = orbs.at[2, 3 + low, half]
        move = pltpu.make_async_remote_copy(
            orb_in.at[to_zp], target, move_send.at[to_zp], move_recv.at[landing],
            device_id=(to, g), device_id_type=MESH)
        moves.append((to, move))
        pl.when(to != me)(move.start)
        pl.when(to == me)(pltpu.make_async_copy(orb_in.at[to_zp], target, move_recv.at[landing]).start)

    for to in others():
        pltpu.make_async_remote_copy(
            rows_in.at[:, to, :], recv.at[:, me, :], row_send, row_recv,
            device_id=(to, g), device_id_type=MESH).start()
    pltpu.make_async_copy(rows_in.at[:, me, :], recv.at[:, me, :], row_recv).start()

    for yl in range(2):
        for h in range(2):
            landed = orbs.at[2, 3 + yl, h]
            pltpu.make_async_copy(landed, landed, move_recv.at[yl * 2 + h]).wait()
    orb_copies = []
    for number, (a, b, y0, ny) in enumerate(ORB_NEIGHBOURS):
        yy = 3 - 2 * b + y0
        orb_copies.append(pltpu.make_async_remote_copy(
            orbs.at[2, 3 + y0 : 3 + y0 + ny], orbs.at[2 - a, yy : yy + ny],
            orb_send.at[number], orb_recv.at[number], device_id=near(a, b), device_id_type=MESH))
        orb_copies[-1].start()

    pltpu.make_async_copy(recv, recv, row_recv).wait()
    for zl in range(2):
        plane = recv[zl].T
        for yl in range(2):
            line = plane[yl * 64 : yl * 64 + 64]
            own[zl, yl] = line
            lines[zl, yl] = line.astype(BF16)
    copies = []
    for number, (a, b, z0, nz, y0, ny) in enumerate(NEIGHBOURS):
        zz, yy = 3 - 2 * a + z0, 3 - 2 * b + y0
        copies.append(pltpu.make_async_remote_copy(
            lines.at[z0 : z0 + nz, y0 : y0 + ny], halo.at[zz : zz + nz, yy : yy + ny],
            halo_send.at[number], halo_recv.at[number], device_id=near(a, b), device_id_type=MESH))
        copies[-1].start()

    for copy in orb_copies:
        copy.wait_recv()
    build_orbitals(orbs, wf, pf)
    build_products(wf, pf, sf, qb)
    build_coefficients(qb, coef)
    place_lines(own, True, vf)
    for copy in copies:
        copy.wait_recv()
    place_lines(halo, False, vf)
    finish(apply_stencil(vf, coef), factor, ug)

    for to in others():
        pltpu.make_async_remote_copy(
            ug.at[:, to, :], back.at[:, me, :], back_send, back_recv,
            device_id=(to, g), device_id_type=MESH).start()
    pltpu.make_async_copy(ug.at[:, me, :], back.at[:, me, :], back_recv).start()
    for copy in orb_copies + copies:
        copy.wait_send()
    for to, move in moves:
        pl.when(to != me)(move.wait_send)
    pltpu.make_async_copy(rows_in.at[:, 0:127, :], rows_in.at[:, 0:127, :], row_send).wait()

    pltpu.make_async_copy(back, back, back_recv).wait()
    parts[0] = jnp.broadcast_to(jnp.sum(back[2], axis=0, keepdims=True), (8, 128))
    part_copies = []
    for step in range(1, 4):
        part_copies.append(pltpu.make_async_remote_copy(
            parts.at[0], parts.at[4 - step], part_send.at[step - 1], part_recv.at[step - 1],
            device_id=(me, (g + step) % 4), device_id_type=MESH))
        part_copies[-1].start()
    for z in range(8):
        for y in range(32):
            source = device_of(z // 2, y)
            out[0, z : z + 1, y * 128 : y * 128 + 128] = back[z % 2, source : source + 1, :]
    for copy in part_copies:
        copy.wait()
    total = None
    for slab in range(4):
        part = parts[(slab - g + 4) % 4]
        total = part if total is None else total + part
    margins[...] = total[0:1]
    pltpu.make_async_copy(ug.at[:, 0:127, :], ug.at[:, 0:127, :], back_send).wait()


def local(potentials, orbitals, energies, local_potential, inverse_factor):
    packed = orbitals.reshape(32, 4, 2, 2, 16).transpose(1, 4, 2, 3, 0).reshape(4, 16, 128)
    vmem = pl.BlockSpec(memory_space=pltpu.VMEM)
    dma = pltpu.SemaphoreType.DMA
    return pl.pallas_call(
        kernel,
        out_shape=(jax.ShapeDtypeStruct((1, 8, 4096), F32), jax.ShapeDtypeStruct((1, 128), F32)),
        in_specs=[vmem] * 5,
        out_specs=(vmem,) * 2,
        scratch_shapes=[
            pltpu.VMEM((2, 128, 128), F32),
            pltpu.VMEM((2, 128, 128), F32),
            pltpu.VMEM((2, 2, 64, 128), BF16),
            pltpu.VMEM((2, 2, 64, 128), F32),
            pltpu.VMEM((8, 8, 64, 128), BF16),
            pltpu.VMEM((5, 8, 2, 16, 128), BF16),
            pltpu.VMEM((3, 128, 128), F32),
            pltpu.VMEM((3, 128, 128), F32),
            pltpu.VMEM((4, 8, 128), F32),
            pltpu.VMEM((5, 48, 128), F32),
            pltpu.VMEM((128, 128), F32),
            pltpu.VMEM((len(LINES), 64, 128), F32),
            pltpu.VMEM((len(ROWS2D), 80, 128), F32),
            pltpu.VMEM((len(ROWS2D), 80, 128), F32),
            pltpu.VMEM((5, 80, 128), F32),
            pltpu.VMEM((COUNT * 64, 256), BF16),
            pltpu.VMEM((COUNT * 64, 512), F32),
            pltpu.VMEM((len(LINES), 80, 128), F32),
            dma, dma, dma((4,)), dma((4,)), dma((12,)), dma((12,)), dma((16,)), dma((16,)),
            dma, dma, dma((3,)), dma((3,)),
        ],
        compiler_params=pltpu.CompilerParams(
            collective_id=0, has_side_effects=True, vmem_limit_bytes=48 * 1024 * 1024),
    )(potentials, packed, energies.reshape(1, 32), local_potential, inverse_factor)


def solution(mesh):
    in_specs = (P("pot", "grid", None), P(None, "grid", "pot"), P(), P(), P())
    out_specs = (P("pot", "grid", None), P("pot", None))
    return jax.shard_map(local, mesh=mesh, in_specs=in_specs, out_specs=out_specs, check_vma=False)
```

```python
import jax
import jax.numpy as jnp
from jax import lax
from jax.experimental import pallas as pl
from jax.experimental.pallas import tpu as pltpu
from jax.sharding import PartitionSpec as P

MESH = pl.DeviceIdType.MESH
F32 = jnp.float32
BF16 = jnp.bfloat16
NZ = 32
NPAIR = 32
ROWS2D = [(dz, dy) for dz in range(-3, 4) for dy in range(-3, 4) if abs(dz) + abs(dy) <= 3]
INDEX2D = {pair: number for number, pair in enumerate(ROWS2D)}
OFFSETS = [
    (dz, dy, dx)
    for dz, dy in ROWS2D
    for dx in range(-3, 4)
    if abs(dz) + abs(dy) + abs(dx) <= 3
]
COUNT = len(OFFSETS)
LINES = sorted({(3 + zl + dz, 3 + yl + dy) for dz, dy in ROWS2D for zl in range(2) for yl in range(2)})
LINE_INDEX = {line: number for number, line in enumerate(LINES)}
CROSS = [(0, 0), (1, 0), (-1, 0), (0, 1), (0, -1)]
FAR = 1e30


def tile_of(p):
    core, x, y, low = p % 2, (p // 2) % 4, (p // 8) % 8, p // 64
    return low * 2 + core, y * 4 + x + (y % 2) * (3 - 2 * x)


def device_of(zp, yt):
    y, s = yt // 4, yt % 4
    return (zp // 2) * 64 + y * 8 + (s + (y % 2) * (3 - 2 * s)) * 2 + zp % 2


def place(zt, yt):
    return device_of(zt % 4, yt), zt // 4


def line_sets(dz, dy):
    return [(3 + zl + dz, 3 + yl + dy) for zl in range(2) for yl in range(2)]


def pack_helpers():
    n = lax.broadcasted_iota(jnp.int32, (512, 256), 0)
    k = lax.broadcasted_iota(jnp.int32, (512, 256), 1)
    want = (n % 32) * 8 + (n // 128) * 2 + (n // 32) % 2
    choose = jnp.where(k == want, 1.0, 0.0).astype(BF16)
    fold = lax.broadcasted_iota(jnp.int32, (16, 32), 1) % 16 == lax.broadcasted_iota(jnp.int32, (16, 32), 0)
    return choose, jnp.where(fold, 1.0, 0.0).astype(BF16)


def pack_orbitals(orb, choose, fold, packed):
    flat = orb[...].astype(F32).reshape(256, 32).astype(BF16)
    lanes = jnp.dot(choose, flat, preferred_element_type=F32)
    row = lax.broadcasted_iota(jnp.int32, (512, 32), 0)
    cell = lax.broadcasted_iota(jnp.int32, (512, 32), 1)
    lanes = jnp.where(cell // 16 == (row // 64) % 2, lanes, 0.0).astype(BF16)
    folded = lax.dot_general(fold, lanes, (((1,), (1,)), ((), ())), preferred_element_type=F32)
    for pair in range(4):
        packed[pair] = folded[:, pair * 128 : pair * 128 + 128].astype(BF16)


def build_weights(zt, yt, columns, energies, pads, ls, bl, wf, sf):
    for m in range(5):
        pp = yt - 2 + m
        ok = jnp.logical_and(pp >= 0, pp < NPAIR)
        pads[m, 0:8, :] = jnp.full((8, 128), FAR, F32)
        pads[m, 40:48, :] = jnp.full((8, 128), FAR, F32)
        pads[m, 8:40, :] = jnp.where(ok, columns[m], FAR)
        ls[m * 8 : m * 8 + 8, :] = pads[m, pl.ds(2 * zt + 5, 8), :]
    lt = ls[...].T
    for number, (k, r) in enumerate(LINES):
        m, yl = (r + 1) // 2, (r + 1) % 2
        c = m * 8 + k
        bl[number] = jnp.broadcast_to(lt[yl * 64 : yl * 64 + 64, c : c + 1], (64, 128))
    group = lax.broadcasted_iota(jnp.int32, (64, 128), 1) // 32
    row = energies[...]
    shift3 = 3.0 - jnp.concatenate([row, row, row, row], axis=1)
    zeros = jnp.zeros((8, 128), F32)
    for number, (dz, dy) in enumerate(ROWS2D):
        at = None
        for l, line in enumerate(line_sets(dz, dy)):
            here = bl[LINE_INDEX[line]]
            at = here if at is None else jnp.where(group == l, here, at)
        wf[number, 0:8, :] = zeros
        wf[number, 72:80, :] = zeros
        wf[number, 8:72, :] = jnp.where(at > 0.1 * FAR, 0.0, 0.4 / (at + shift3))
    for number, (dz, dy) in enumerate(CROSS):
        i = INDEX2D[(dz, dy)]
        total = wf[i, 3:75, :] + wf[i, 5:77, :]
        for ez, ey in CROSS[1:]:
            total = total + wf[INDEX2D[(dz + ez, dy + ey)], 4:76, :]
        sf[number, 4:76, :] = total


def build_orbitals(orbs, wf, pf):
    group = lax.broadcasted_iota(jnp.int32, (16, 128), 1) // 32
    zeros = jnp.zeros((8, 128), F32)
    for number, (dz, dy) in enumerate(ROWS2D):
        pf[number, 0:8, :] = zeros
        pf[number, 72:80, :] = zeros
        for h in range(2):
            for xq in range(2):
                orb = None
                for l, (k, r) in enumerate(line_sets(dz, dy)):
                    q, zl = (k + 1) // 2, (k + 1) % 2
                    unit = orbs[q, r, h].astype(F32)
                    shift = (l * 32 - xq * 64 - zl * 32) % 128
                    if shift:
                        unit = pltpu.roll(unit, shift, 1)
                    orb = unit if orb is None else jnp.where(group == l, unit, orb)
                x0 = 8 + h * 32 + xq * 16
                pf[number, x0 : x0 + 16, :] = orb * wf[number, x0 : x0 + 16, :]


def build_products(wf, pf, sf, qb):
    def w(dz, dy, dx):
        return wf[INDEX2D[(dz, dy)], 8 + dx : 72 + dx, :]

    def s1(dz, dy, dx):
        return sf[CROSS.index((dz, dy)), 8 + dx : 72 + dx, :]

    def unit(axis, sign):
        return tuple(sign if a == axis else 0 for a in range(3))

    def plus(a, b):
        return tuple(x + y for x, y in zip(a, b))

    mine = -0.25 * pf[INDEX2D[(0, 0)], 8:72, :]
    for number, offset in enumerate(OFFSETS):
        dist = sum(abs(c) for c in offset)
        steps = []
        for axis in range(3):
            if offset[axis]:
                steps.append((unit(axis, 1 if offset[axis] > 0 else -1), abs(offset[axis])))
        if dist == 0:
            orb = 1.248 / w(0, 0, 0)
            path = orb + 1.6 * s1(0, 0, 0)
        elif dist == 1:
            e = offset
            w0, we = w(0, 0, 0), w(*e)
            path = 1.52 + w0 * (s1(0, 0, 0) - we) + we * s1(*e)
            for axis in range(3):
                if not e[axis]:
                    for sign in (1, -1):
                        b = unit(axis, sign)
                        path = path + w(*b) * w(*plus(b, e))
        elif dist == 2:
            if len(steps) == 1:
                path = 1.6 * w(*steps[0][0])
            else:
                path = 1.6 * (w(*steps[0][0]) + w(*steps[1][0]))
        elif len(steps) == 1:
            a = steps[0][0]
            path = w(*a) * w(*plus(a, a))
        elif len(steps) == 2:
            (a, b) = (steps[0][0], steps[1][0]) if steps[0][1] == 2 else (steps[1][0], steps[0][0])
            ab = w(*plus(a, b))
            path = w(*a) * (w(*plus(a, a)) + ab) + w(*b) * ab
        else:
            a, b, c = (s[0] for s in steps)
            ab, ac, bc = w(*plus(a, b)), w(*plus(a, c)), w(*plus(b, c))
            path = w(*a) * (ab + ac) + w(*b) * (ab + bc) + w(*c) * (ac + bc)
        dz, dy, dx = offset
        q = mine * pf[INDEX2D[(dz, dy)], 8 + dx : 72 + dx, :] * path
        high = q.astype(BF16)
        qb[number * 64 : number * 64 + 64, 0:128] = high
        qb[number * 64 : number * 64 + 64, 128:256] = (q - high.astype(F32)).astype(BF16)


def build_coefficients(qb, coef):
    k = lax.broadcasted_iota(jnp.int32, (256, 512), 0)
    n = lax.broadcasted_iota(jnp.int32, (256, 512), 1)
    spread = jnp.where((k % 128) // 32 == n // 128, 1.0, 0.0).astype(BF16)

    @pl.loop(0, 9)
    def _(step):
        rows = pl.ds(pl.multiple_of(step * 448, 448), 448)
        coef[rows, :] = jnp.dot(qb[rows, :], spread, preferred_element_type=F32)


def place_lines(source, inside, vf):
    zeros = jnp.zeros((8, 128), F32)
    for number, (k, r) in enumerate(LINES):
        here = 3 <= k <= 4 and 3 <= r <= 4
        if here != inside:
            continue
        vf[number, 0:8, :] = zeros
        vf[number, 72:80, :] = zeros
        vf[number, 8:72, :] = source[k - 3, r - 3] if here else source[k, r].astype(F32)


def apply_stencil(vf, coef):
    trial = []
    for l in range(4):
        zl, yl = l // 2, l % 2
        total = vf[LINE_INDEX[(3 + zl, 3 + yl)], 8:72, :]
        for number, (dz, dy, dx) in enumerate(OFFSETS):
            field = vf[LINE_INDEX[(3 + zl + dz, 3 + yl + dy)], 8 + dx : 72 + dx, :]
            total = total + coef[number * 64 : number * 64 + 64, l * 128 : l * 128 + 128] * field
        trial.append(total)
    return trial


def pots_by_cells(trial):
    columns = []
    for zl in range(2):
        plane = jnp.concatenate([trial[2 * zl], trial[2 * zl + 1]], axis=0)
        columns.append(plane.T.astype(BF16))
    return columns


def gram_part(columns):
    gram = None
    for part in columns:
        part = lax.dot_general(part, part, (((1,), (1,)), ((), ())), preferred_element_type=F32)
        gram = part if gram is None else gram + part
    return gram * (1.0 / 131072.0)


NEIGHBOURS = [
    (1, 1, 1, 1, 0, 2), (1, -1, 1, 1, 0, 2), (-1, 1, 0, 1, 0, 2), (-1, -1, 0, 1, 0, 2),
    (1, 1, 0, 1, 1, 1), (1, -1, 0, 1, 0, 1), (-1, 1, 1, 1, 1, 1), (-1, -1, 1, 1, 0, 1),
    (0, 2, 0, 2, 1, 1), (0, -2, 0, 2, 0, 1), (2, 0, 1, 1, 0, 2), (-2, 0, 0, 1, 0, 2),
    (0, 1, 0, 2, 0, 2), (0, -1, 0, 2, 0, 2), (1, 0, 0, 2, 0, 2), (-1, 0, 0, 2, 0, 2),
]
ORB_NEIGHBOURS = [
    (1, 0, 0, 2), (-1, 0, 0, 2), (0, 1, 0, 2), (0, -1, 0, 2), (2, 0, 0, 2), (-2, 0, 0, 2),
    (1, 1, 0, 2), (1, -1, 0, 2), (-1, 1, 0, 2), (-1, -1, 0, 2), (0, 2, 1, 1), (0, -2, 0, 1),
]


def ring(distance, size):
    return min(distance, size - distance)


OTHERS = sorted(
    ((y, x, z, c) for y in range(8) for x in range(4) for z in range(2) for c in range(2) if y or x or z or c),
    key=lambda d: (-(ring(d[0], 8) + ring(d[1], 4) + d[2]), d),
)


def kernel(pot_far, orb_far, energies_far, loc_far, factor_far, out, margins,
           orb, energies, columns, factor, orb_in, recv, lines, own, halo, orbs, gram, gram_back, ug, parts, pads, ls, bl, wf, pf, sf, qb, coef, vf,
           row_send, row_recv, move_send, move_recv, orb_send, orb_recv, halo_send, halo_recv,
           gram_send, gram_recv, back_send, back_recv, part_send, part_recv, load_sem):
    me, g = lax.axis_index("pot"), lax.axis_index("grid")
    zp, yt = tile_of(me)
    zt = g * 4 + zp
    ys = [(me // 8 + d) % 8 * 8 for d in range(8)]
    xs = [(me // 2 + d) % 4 * 2 for d in range(4)]
    zs = [me // 64 * 64, (1 - me // 64) * 64]
    cs = [me % 2, 1 - me % 2]

    def others():
        for y, x, z, c in OTHERS:
            yield ys[y] + xs[x] + zs[z] + cs[c]

    def cells_of(y, x, z, c):
        across = ys[y] // 8 % 2
        to_yt = ys[y] // 2 + xs[x] // 2 + across * (3 - xs[x])
        to_plane = zs[z] // 16 + cs[c] * 2
        return pot_far.at[0, pl.ds(to_plane, 2), pl.ds(pl.multiple_of(to_yt * 128, 128), 128)]

    def near(a, b):
        return place((zt + a + 16) % 16, (yt + b + 32) % 32)

    loads = [
        pltpu.make_async_copy(orb_far, orb, load_sem.at[0]),
        pltpu.make_async_copy(energies_far, energies, load_sem.at[1]),
        pltpu.make_async_copy(factor_far, factor, load_sem.at[2]),
    ]
    for m in range(5):
        at = pl.multiple_of(jnp.clip(yt - 2 + m, 0, NPAIR - 1) * 128, 128)
        loads.append(pltpu.make_async_copy(loc_far.at[:, pl.ds(at, 128)], columns.at[m], load_sem.at[3 + m]))
    for load in loads:
        load.start()

    barrier = pltpu.get_barrier_semaphore()
    for to in others():
        pl.semaphore_signal(barrier, inc=1, device_id=(to, g), device_id_type=MESH)
    for step in range(1, 4):
        pl.semaphore_signal(barrier, inc=1, device_id=(me, (g + step) % 4), device_id_type=MESH)
    for a, b, *_ in ORB_NEIGHBOURS:
        pl.semaphore_signal(barrier, inc=1, device_id=near(a, b), device_id_type=MESH)

    choose, fold = pack_helpers()
    loads[0].wait()
    pack_orbitals(orb, choose, fold, orb_in)
    pl.semaphore_wait(barrier, len(OTHERS) + 3 + len(ORB_NEIGHBOURS))

    row, half = me // 2, me % 2
    low, landing = row % 2, (row % 2) * 2 + half
    moves = []
    for to_zp in range(4):
        to = device_of(to_zp, row // 2)
        target = orbs.at[2, 3 + low, half]
        move = pltpu.make_async_remote_copy(
            orb_in.at[to_zp], target, move_send.at[to_zp], move_recv.at[landing],
            device_id=(to, g), device_id_type=MESH)
        moves.append((to, move))
        pl.when(to != me)(move.start)
        pl.when(to == me)(pltpu.make_async_copy(orb_in.at[to_zp], target, move_recv.at[landing]).start)

    for to, offsets in zip(others(), OTHERS):
        pltpu.make_async_remote_copy(
            cells_of(*offsets), recv.at[:, me, :], row_send, row_recv,
            device_id=(to, g), device_id_type=MESH).start()
    pltpu.make_async_copy(cells_of(0, 0, 0, 0), recv.at[:, me, :], row_recv).start()

    for load in loads[1:]:
        load.wait()
    build_weights(zt, yt, columns, energies, pads, ls, bl, wf, sf)

    for yl in range(2):
        for h in range(2):
            landed = orbs.at[2, 3 + yl, h]
            pltpu.make_async_copy(landed, landed, move_recv.at[yl * 2 + h]).wait()
    orb_copies = []
    for number, (a, b, y0, ny) in enumerate(ORB_NEIGHBOURS):
        yy = 3 - 2 * b + y0
        orb_copies.append(pltpu.make_async_remote_copy(
            orbs.at[2, 3 + y0 : 3 + y0 + ny], orbs.at[2 - a, yy : yy + ny],
            orb_send.at[number], orb_recv.at[number], device_id=near(a, b), device_id_type=MESH))
        orb_copies[-1].start()

    pltpu.make_async_copy(recv, recv, row_recv).wait()
    for zl in range(2):
        plane = recv[zl].T
        for yl in range(2):
            line = plane[yl * 64 : yl * 64 + 64]
            own[zl, yl] = line
            lines[zl, yl] = line.astype(BF16)
    copies = []
    for number, (a, b, z0, nz, y0, ny) in enumerate(NEIGHBOURS):
        zz, yy = 3 - 2 * a + z0, 3 - 2 * b + y0
        copies.append(pltpu.make_async_remote_copy(
            lines.at[z0 : z0 + nz, y0 : y0 + ny], halo.at[zz : zz + nz, yy : yy + ny],
            halo_send.at[number], halo_recv.at[number], device_id=near(a, b), device_id_type=MESH))
        copies[-1].start()

    for copy in orb_copies:
        copy.wait_recv()
    build_orbitals(orbs, wf, pf)
    build_products(wf, pf, sf, qb)
    build_coefficients(qb, coef)
    place_lines(own, True, vf)
    for copy in copies:
        copy.wait_recv()
    place_lines(halo, False, vf)
    columns = pots_by_cells(apply_stencil(vf, coef))

    gram[0] = gram_part(columns)
    for to in others():
        pltpu.make_async_remote_copy(
            gram.at[:, to, :], gram_back.at[:, me, :], gram_send, gram_recv,
            device_id=(to, g), device_id_type=MESH).start()
    pltpu.make_async_copy(gram.at[:, me, :], gram_back.at[:, me, :], gram_recv).start()
    for zl in range(2):
        ug[zl] = jnp.dot(factor[...], columns[zl], preferred_element_type=F32)
    cells = out.at[0, pl.ds(zp * 2, 2), pl.ds(pl.multiple_of(yt * 128, 128), 128)]
    for to in others():
        pltpu.make_async_remote_copy(
            ug.at[:, to, :], cells, back_send, back_recv, device_id=(to, g), device_id_type=MESH).start()
    pltpu.make_async_copy(ug.at[:, me, :], cells, back_recv).start()

    pltpu.make_async_copy(gram_back, gram_back, gram_recv).wait()
    parts[0] = jnp.broadcast_to(jnp.sum(gram_back[0], axis=0, keepdims=True), (8, 128))
    part_copies = []
    for step in range(1, 4):
        part_copies.append(pltpu.make_async_remote_copy(
            parts.at[0], parts.at[4 - step], part_send.at[step - 1], part_recv.at[step - 1],
            device_id=(me, (g + step) % 4), device_id_type=MESH))
        part_copies[-1].start()
    for copy in orb_copies + copies:
        copy.wait_send()
    for to, move in moves:
        pl.when(to != me)(move.wait_send)
    pltpu.make_async_copy(recv.at[:, 0:127, :], recv.at[:, 0:127, :], row_send).wait()

    for copy in part_copies:
        copy.wait()
    total = None
    for slab in range(4):
        part = parts[(slab - g + 4) % 4]
        total = part if total is None else total + part
    margins[...] = total[0:1]
    pltpu.make_async_copy(out, out, back_recv).wait()
    pltpu.make_async_copy(ug.at[:, 0:127, :], ug.at[:, 0:127, :], back_send).wait()
    pltpu.make_async_copy(gram.at[:, 0:127, :], gram.at[:, 0:127, :], gram_send).wait()


def local(potentials, orbitals, energies, local_potential, inverse_factor):
    hbm = pl.BlockSpec(memory_space=pltpu.HBM)
    vmem = pl.BlockSpec(memory_space=pltpu.VMEM)
    dma = pltpu.SemaphoreType.DMA
    return pl.pallas_call(
        kernel,
        out_shape=(jax.ShapeDtypeStruct((1, 8, 4096), F32), jax.ShapeDtypeStruct((1, 128), F32)),
        in_specs=[hbm] * 5,
        out_specs=(hbm, vmem),
        scratch_shapes=[
            pltpu.VMEM((32, 8, 32), BF16),
            pltpu.VMEM((1, 32), F32),
            pltpu.VMEM((5, 32, 128), F32),
            pltpu.VMEM((128, 128), BF16),
            pltpu.VMEM((4, 16, 128), BF16),
            pltpu.VMEM((2, 128, 128), F32),
            pltpu.VMEM((2, 2, 64, 128), BF16),
            pltpu.VMEM((2, 2, 64, 128), F32),
            pltpu.VMEM((8, 8, 64, 128), BF16),
            pltpu.VMEM((5, 8, 2, 16, 128), BF16),
            pltpu.VMEM((1, 128, 128), F32),
            pltpu.VMEM((1, 128, 128), F32),
            pltpu.VMEM((2, 128, 128), F32),
            pltpu.VMEM((4, 8, 128), F32),
            pltpu.VMEM((5, 48, 128), F32),
            pltpu.VMEM((128, 128), F32),
            pltpu.VMEM((len(LINES), 64, 128), F32),
            pltpu.VMEM((len(ROWS2D), 80, 128), F32),
            pltpu.VMEM((len(ROWS2D), 80, 128), F32),
            pltpu.VMEM((5, 80, 128), F32),
            pltpu.VMEM((COUNT * 64, 256), BF16),
            pltpu.VMEM((COUNT * 64, 512), F32),
            pltpu.VMEM((len(LINES), 80, 128), F32),
            dma, dma, dma((4,)), dma((4,)), dma((12,)), dma((12,)), dma((16,)), dma((16,)),
            dma, dma, dma, dma, dma((3,)), dma((3,)), dma((8,)),
        ],
        compiler_params=pltpu.CompilerParams(
            collective_id=0, has_side_effects=True, vmem_limit_bytes=58 * 1024 * 1024),
    )(potentials, orbitals, energies.reshape(1, 32), local_potential, inverse_factor)


def solution(mesh):
    in_specs = (P("pot", "grid", None), P(None, "grid", "pot"), P(), P(), P())
    out_specs = (P("pot", "grid", None), P("pot", None))
    return jax.shard_map(local, mesh=mesh, in_specs=in_specs, out_specs=out_specs, check_vma=False)
```

```python
import jax
import jax.numpy as jnp
from jax import lax
from jax.experimental import pallas as pl
from jax.experimental.pallas import tpu as pltpu
from jax.sharding import PartitionSpec as P

MESH = pl.DeviceIdType.MESH
F32 = jnp.float32
BF16 = jnp.bfloat16
NZ = 32
NPAIR = 32
ROWS2D = [(dz, dy) for dz in range(-3, 4) for dy in range(-3, 4) if abs(dz) + abs(dy) <= 3]
INDEX2D = {pair: number for number, pair in enumerate(ROWS2D)}
OFFSETS = [
    (dz, dy, dx)
    for dz, dy in ROWS2D
    for dx in range(-3, 4)
    if abs(dz) + abs(dy) + abs(dx) <= 3
]
COUNT = len(OFFSETS)
LINES = sorted({(3 + zl + dz, 3 + yl + dy) for dz, dy in ROWS2D for zl in range(2) for yl in range(2)})
LINE_INDEX = {line: number for number, line in enumerate(LINES)}
CROSS = [(0, 0), (1, 0), (-1, 0), (0, 1), (0, -1)]
FAR = 1e30


def tile_of(p):
    core, x, y, low = p % 2, (p // 2) % 4, (p // 8) % 8, p // 64
    return low * 2 + core, y * 4 + x + (y % 2) * (3 - 2 * x)


def device_of(zp, yt):
    y, s = yt // 4, yt % 4
    return (zp // 2) * 64 + y * 8 + (s + (y % 2) * (3 - 2 * s)) * 2 + zp % 2


def place(zt, yt):
    return device_of(zt % 4, yt), zt // 4


def line_sets(dz, dy):
    return [(3 + zl + dz, 3 + yl + dy) for zl in range(2) for yl in range(2)]


def pack_helpers():
    n = lax.broadcasted_iota(jnp.int32, (512, 256), 0)
    k = lax.broadcasted_iota(jnp.int32, (512, 256), 1)
    want = (n % 32) * 8 + (n // 128) * 2 + (n // 32) % 2
    choose = jnp.where(k == want, 1.0, 0.0).astype(BF16)
    fold = lax.broadcasted_iota(jnp.int32, (16, 32), 1) % 16 == lax.broadcasted_iota(jnp.int32, (16, 32), 0)
    return choose, jnp.where(fold, 1.0, 0.0).astype(BF16)


def pack_orbitals(orb, choose, fold, packed):
    flat = orb[...].astype(F32).reshape(256, 32).astype(BF16)
    lanes = jnp.dot(choose, flat, preferred_element_type=F32)
    row = lax.broadcasted_iota(jnp.int32, (512, 32), 0)
    cell = lax.broadcasted_iota(jnp.int32, (512, 32), 1)
    lanes = jnp.where(cell // 16 == (row // 64) % 2, lanes, 0.0).astype(BF16)
    folded = lax.dot_general(fold, lanes, (((1,), (1,)), ((), ())), preferred_element_type=F32)
    for pair in range(4):
        packed[pair] = folded[:, pair * 128 : pair * 128 + 128].astype(BF16)


def build_weights(zt, yt, columns, energies, pads, ls, bl, wf, sf):
    for m in range(5):
        pp = yt - 2 + m
        ok = jnp.logical_and(pp >= 0, pp < NPAIR)
        pads[m, 0:8, :] = jnp.full((8, 128), FAR, F32)
        pads[m, 40:48, :] = jnp.full((8, 128), FAR, F32)
        pads[m, 8:40, :] = jnp.where(ok, columns[m], FAR)
        ls[m * 8 : m * 8 + 8, :] = pads[m, pl.ds(2 * zt + 5, 8), :]
    lt = ls[...].T
    for number, (k, r) in enumerate(LINES):
        m, yl = (r + 1) // 2, (r + 1) % 2
        c = m * 8 + k
        bl[number] = jnp.broadcast_to(lt[yl * 64 : yl * 64 + 64, c : c + 1], (64, 128))
    group = lax.broadcasted_iota(jnp.int32, (64, 128), 1) // 32
    row = energies[...]
    shift3 = 3.0 - jnp.concatenate([row, row, row, row], axis=1)
    zeros = jnp.zeros((8, 128), F32)
    for number, (dz, dy) in enumerate(ROWS2D):
        at = None
        for l, line in enumerate(line_sets(dz, dy)):
            here = bl[LINE_INDEX[line]]
            at = here if at is None else jnp.where(group == l, here, at)
        wf[number, 0:8, :] = zeros
        wf[number, 72:80, :] = zeros
        wf[number, 8:72, :] = jnp.where(at > 0.1 * FAR, 0.0, 0.4 / (at + shift3))
    for number, (dz, dy) in enumerate(CROSS):
        i = INDEX2D[(dz, dy)]
        total = wf[i, 3:75, :] + wf[i, 5:77, :]
        for ez, ey in CROSS[1:]:
            total = total + wf[INDEX2D[(dz + ez, dy + ey)], 4:76, :]
        sf[number, 4:76, :] = total


def build_orbitals(orbs, wf, pf):
    group = lax.broadcasted_iota(jnp.int32, (16, 128), 1) // 32
    zeros = jnp.zeros((8, 128), F32)
    for number, (dz, dy) in enumerate(ROWS2D):
        pf[number, 0:8, :] = zeros
        pf[number, 72:80, :] = zeros
        for h in range(2):
            for xq in range(2):
                orb = None
                for l, (k, r) in enumerate(line_sets(dz, dy)):
                    q, zl = (k + 1) // 2, (k + 1) % 2
                    unit = orbs[q, r, h].astype(F32)
                    shift = (l * 32 - xq * 64 - zl * 32) % 128
                    if shift:
                        unit = pltpu.roll(unit, shift, 1)
                    orb = unit if orb is None else jnp.where(group == l, unit, orb)
                x0 = 8 + h * 32 + xq * 16
                pf[number, x0 : x0 + 16, :] = orb * wf[number, x0 : x0 + 16, :]


def build_products(wf, pf, sf, qb):
    def w(dz, dy, dx):
        return wf[INDEX2D[(dz, dy)], 8 + dx : 72 + dx, :]

    def s1(dz, dy, dx):
        return sf[CROSS.index((dz, dy)), 8 + dx : 72 + dx, :]

    def unit(axis, sign):
        return tuple(sign if a == axis else 0 for a in range(3))

    def plus(a, b):
        return tuple(x + y for x, y in zip(a, b))

    mine = -0.25 * pf[INDEX2D[(0, 0)], 8:72, :]
    for number, offset in enumerate(OFFSETS):
        dist = sum(abs(c) for c in offset)
        steps = []
        for axis in range(3):
            if offset[axis]:
                steps.append((unit(axis, 1 if offset[axis] > 0 else -1), abs(offset[axis])))
        if dist == 0:
            orb = 1.248 / w(0, 0, 0)
            path = orb + 1.6 * s1(0, 0, 0)
        elif dist == 1:
            e = offset
            w0, we = w(0, 0, 0), w(*e)
            path = 1.52 + w0 * (s1(0, 0, 0) - we) + we * s1(*e)
            for axis in range(3):
                if not e[axis]:
                    for sign in (1, -1):
                        b = unit(axis, sign)
                        path = path + w(*b) * w(*plus(b, e))
        elif dist == 2:
            if len(steps) == 1:
                path = 1.6 * w(*steps[0][0])
            else:
                path = 1.6 * (w(*steps[0][0]) + w(*steps[1][0]))
        elif len(steps) == 1:
            a = steps[0][0]
            path = w(*a) * w(*plus(a, a))
        elif len(steps) == 2:
            (a, b) = (steps[0][0], steps[1][0]) if steps[0][1] == 2 else (steps[1][0], steps[0][0])
            ab = w(*plus(a, b))
            path = w(*a) * (w(*plus(a, a)) + ab) + w(*b) * ab
        else:
            a, b, c = (s[0] for s in steps)
            ab, ac, bc = w(*plus(a, b)), w(*plus(a, c)), w(*plus(b, c))
            path = w(*a) * (ab + ac) + w(*b) * (ab + bc) + w(*c) * (ac + bc)
        dz, dy, dx = offset
        q = mine * pf[INDEX2D[(dz, dy)], 8 + dx : 72 + dx, :] * path
        high = q.astype(BF16)
        qb[number * 64 : number * 64 + 64, 0:128] = high
        qb[number * 64 : number * 64 + 64, 128:256] = (q - high.astype(F32)).astype(BF16)


def build_coefficients(qb, coef):
    k = lax.broadcasted_iota(jnp.int32, (256, 512), 0)
    n = lax.broadcasted_iota(jnp.int32, (256, 512), 1)
    spread = jnp.where((k % 128) // 32 == n // 128, 1.0, 0.0).astype(BF16)

    @pl.loop(0, 9)
    def _(step):
        rows = pl.ds(pl.multiple_of(step * 448, 448), 448)
        coef[rows, :] = jnp.dot(qb[rows, :], spread, preferred_element_type=F32)


def place_lines(source, inside, vf):
    zeros = jnp.zeros((8, 128), F32)
    for number, (k, r) in enumerate(LINES):
        here = 3 <= k <= 4 and 3 <= r <= 4
        if here != inside:
            continue
        vf[number, 0:8, :] = zeros
        vf[number, 72:80, :] = zeros
        vf[number, 8:72, :] = source[k - 3, r - 3] if here else source[k, r].astype(F32)


def apply_stencil(vf, coef):
    trial = []
    for l in range(4):
        zl, yl = l // 2, l % 2
        total = vf[LINE_INDEX[(3 + zl, 3 + yl)], 8:72, :]
        for number, (dz, dy, dx) in enumerate(OFFSETS):
            field = vf[LINE_INDEX[(3 + zl + dz, 3 + yl + dy)], 8 + dx : 72 + dx, :]
            total = total + coef[number * 64 : number * 64 + 64, l * 128 : l * 128 + 128] * field
        trial.append(total)
    return trial


def pots_by_cells(trial):
    columns = []
    for zl in range(2):
        plane = jnp.concatenate([trial[2 * zl], trial[2 * zl + 1]], axis=0)
        columns.append(plane.T.astype(BF16))
    return columns


def gram_part(columns):
    gram = None
    for part in columns:
        part = lax.dot_general(part, part, (((1,), (1,)), ((), ())), preferred_element_type=F32)
        gram = part if gram is None else gram + part
    return gram * (1.0 / 131072.0)


NEIGHBOURS = [
    (1, 1, 1, 1, 0, 2), (1, -1, 1, 1, 0, 2), (-1, 1, 0, 1, 0, 2), (-1, -1, 0, 1, 0, 2),
    (1, 1, 0, 1, 1, 1), (1, -1, 0, 1, 0, 1), (-1, 1, 1, 1, 1, 1), (-1, -1, 1, 1, 0, 1),
    (0, 2, 0, 2, 1, 1), (0, -2, 0, 2, 0, 1), (2, 0, 1, 1, 0, 2), (-2, 0, 0, 1, 0, 2),
    (0, 1, 0, 2, 0, 2), (0, -1, 0, 2, 0, 2), (1, 0, 0, 2, 0, 2), (-1, 0, 0, 2, 0, 2),
]
ORB_NEIGHBOURS = [
    (1, 0, 0, 2), (-1, 0, 0, 2), (0, 1, 0, 2), (0, -1, 0, 2), (2, 0, 0, 2), (-2, 0, 0, 2),
    (1, 1, 0, 2), (1, -1, 0, 2), (-1, 1, 0, 2), (-1, -1, 0, 2), (0, 2, 1, 1), (0, -2, 0, 1),
]


def ring(distance, size):
    return min(distance, size - distance)


OTHERS = sorted(
    ((y, x, z, c) for y in range(8) for x in range(4) for z in range(2) for c in range(2) if y or x or z or c),
    key=lambda d: (-(ring(d[0], 8) + ring(d[1], 4) + d[2]), d),
)


def kernel(pot_far, orb_far, energies_far, loc_far, factor_far, out, margins,
           orb, energies, columns, factor, orb_in, recv, lines, own, halo, orbs, gram, gram_back, ug, parts, pads, ls, bl, wf, pf, sf, qb, coef, vf,
           row_send, row_recv, move_send, move_recv, orb_send, orb_recv, halo_send, halo_recv,
           gram_send, gram_recv, back_send, back_recv, part_send, part_recv, load_sem):
    me, g = lax.axis_index("pot"), lax.axis_index("grid")
    zp, yt = tile_of(me)
    zt = g * 4 + zp
    ys = [(me // 8 + d) % 8 * 8 for d in range(8)]
    xs = [(me // 2 + d) % 4 * 2 for d in range(4)]
    zs = [me // 64 * 64, (1 - me // 64) * 64]
    cs = [me % 2, 1 - me % 2]

    def others():
        for y, x, z, c in OTHERS:
            yield ys[y] + xs[x] + zs[z] + cs[c]

    def cells_of(y, x, z, c):
        across = ys[y] // 8 % 2
        to_yt = ys[y] // 2 + xs[x] // 2 + across * (3 - xs[x])
        to_plane = zs[z] // 16 + cs[c] * 2
        return pot_far.at[0, pl.ds(to_plane, 2), pl.ds(pl.multiple_of(to_yt * 128, 128), 128)]

    def near(a, b):
        return place((zt + a + 16) % 16, (yt + b + 32) % 32)

    loads = [
        pltpu.make_async_copy(orb_far, orb, load_sem.at[0]),
        pltpu.make_async_copy(energies_far, energies, load_sem.at[1]),
        pltpu.make_async_copy(factor_far, factor, load_sem.at[2]),
    ]
    for m in range(5):
        at = pl.multiple_of(jnp.clip(yt - 2 + m, 0, NPAIR - 1) * 128, 128)
        loads.append(pltpu.make_async_copy(loc_far.at[:, pl.ds(at, 128)], columns.at[m], load_sem.at[3 + m]))
    for load in loads:
        load.start()

    barrier = pltpu.get_barrier_semaphore()
    for to in others():
        pl.semaphore_signal(barrier, inc=1, device_id=(to, g), device_id_type=MESH)
    for step in range(1, 4):
        pl.semaphore_signal(barrier, inc=1, device_id=(me, (g + step) % 4), device_id_type=MESH)
    for a, b, *_ in ORB_NEIGHBOURS:
        pl.semaphore_signal(barrier, inc=1, device_id=near(a, b), device_id_type=MESH)

    choose, fold = pack_helpers()
    loads[0].wait()
    pack_orbitals(orb, choose, fold, orb_in)
    pl.semaphore_wait(barrier, len(OTHERS) + 3 + len(ORB_NEIGHBOURS))

    row, half = me // 2, me % 2
    low, landing = row % 2, (row % 2) * 2 + half
    moves = []
    for to_zp in range(4):
        to = device_of(to_zp, row // 2)
        target = orbs.at[2, 3 + low, half]
        move = pltpu.make_async_remote_copy(
            orb_in.at[to_zp], target, move_send.at[to_zp], move_recv.at[landing],
            device_id=(to, g), device_id_type=MESH)
        moves.append((to, move))
        pl.when(to != me)(move.start)
        pl.when(to == me)(pltpu.make_async_copy(orb_in.at[to_zp], target, move_recv.at[landing]).start)

    for to, offsets in zip(others(), OTHERS):
        pltpu.make_async_remote_copy(
            cells_of(*offsets), recv.at[:, me, :], row_send, row_recv,
            device_id=(to, g), device_id_type=MESH).start()
    pltpu.make_async_copy(cells_of(0, 0, 0, 0), recv.at[:, me, :], row_recv).start()

    for yl in range(2):
        for h in range(2):
            landed = orbs.at[2, 3 + yl, h]
            pltpu.make_async_copy(landed, landed, move_recv.at[yl * 2 + h]).wait()
    orb_copies = []
    for number, (a, b, y0, ny) in enumerate(ORB_NEIGHBOURS):
        yy = 3 - 2 * b + y0
        orb_copies.append(pltpu.make_async_remote_copy(
            orbs.at[2, 3 + y0 : 3 + y0 + ny], orbs.at[2 - a, yy : yy + ny],
            orb_send.at[number], orb_recv.at[number], device_id=near(a, b), device_id_type=MESH))
        orb_copies[-1].start()

    pltpu.make_async_copy(recv, recv, row_recv).wait()
    for zl in range(2):
        plane = recv[zl].T
        for yl in range(2):
            line = plane[yl * 64 : yl * 64 + 64]
            own[zl, yl] = line
            lines[zl, yl] = line.astype(BF16)
    copies = []
    for number, (a, b, z0, nz, y0, ny) in enumerate(NEIGHBOURS):
        zz, yy = 3 - 2 * a + z0, 3 - 2 * b + y0
        copies.append(pltpu.make_async_remote_copy(
            lines.at[z0 : z0 + nz, y0 : y0 + ny], halo.at[zz : zz + nz, yy : yy + ny],
            halo_send.at[number], halo_recv.at[number], device_id=near(a, b), device_id_type=MESH))
        copies[-1].start()

    for load in loads[1:]:
        load.wait()
    build_weights(zt, yt, columns, energies, pads, ls, bl, wf, sf)

    for copy in orb_copies:
        copy.wait_recv()
    build_orbitals(orbs, wf, pf)
    build_products(wf, pf, sf, qb)
    build_coefficients(qb, coef)
    place_lines(own, True, vf)
    for copy in copies:
        copy.wait_recv()
    place_lines(halo, False, vf)
    columns = pots_by_cells(apply_stencil(vf, coef))

    gram[0] = gram_part(columns)
    for to in others():
        pltpu.make_async_remote_copy(
            gram.at[:, to, :], gram_back.at[:, me, :], gram_send, gram_recv,
            device_id=(to, g), device_id_type=MESH).start()
    pltpu.make_async_copy(gram.at[:, me, :], gram_back.at[:, me, :], gram_recv).start()
    for zl in range(2):
        ug[zl] = jnp.dot(factor[...], columns[zl], preferred_element_type=F32)
    cells = out.at[0, pl.ds(zp * 2, 2), pl.ds(pl.multiple_of(yt * 128, 128), 128)]
    for to in others():
        pltpu.make_async_remote_copy(
            ug.at[:, to, :], cells, back_send, back_recv, device_id=(to, g), device_id_type=MESH).start()
    pltpu.make_async_copy(ug.at[:, me, :], cells, back_recv).start()

    pltpu.make_async_copy(gram_back, gram_back, gram_recv).wait()
    parts[0] = jnp.broadcast_to(jnp.sum(gram_back[0], axis=0, keepdims=True), (8, 128))
    part_copies = []
    for step in range(1, 4):
        part_copies.append(pltpu.make_async_remote_copy(
            parts.at[0], parts.at[4 - step], part_send.at[step - 1], part_recv.at[step - 1],
            device_id=(me, (g + step) % 4), device_id_type=MESH))
        part_copies[-1].start()
    for copy in orb_copies + copies:
        copy.wait_send()
    for to, move in moves:
        pl.when(to != me)(move.wait_send)
    pltpu.make_async_copy(recv.at[:, 0:127, :], recv.at[:, 0:127, :], row_send).wait()

    for copy in part_copies:
        copy.wait()
    total = None
    for slab in range(4):
        part = parts[(slab - g + 4) % 4]
        total = part if total is None else total + part
    margins[...] = total[0:1]
    pltpu.make_async_copy(out, out, back_recv).wait()
    pltpu.make_async_copy(ug.at[:, 0:127, :], ug.at[:, 0:127, :], back_send).wait()
    pltpu.make_async_copy(gram.at[:, 0:127, :], gram.at[:, 0:127, :], gram_send).wait()


def local(potentials, orbitals, energies, local_potential, inverse_factor):
    hbm = pl.BlockSpec(memory_space=pltpu.HBM)
    vmem = pl.BlockSpec(memory_space=pltpu.VMEM)
    dma = pltpu.SemaphoreType.DMA
    return pl.pallas_call(
        kernel,
        out_shape=(jax.ShapeDtypeStruct((1, 8, 4096), F32), jax.ShapeDtypeStruct((1, 128), F32)),
        in_specs=[hbm] * 5,
        out_specs=(hbm, vmem),
        scratch_shapes=[
            pltpu.VMEM((32, 8, 32), BF16),
            pltpu.VMEM((1, 32), F32),
            pltpu.VMEM((5, 32, 128), F32),
            pltpu.VMEM((128, 128), BF16),
            pltpu.VMEM((4, 16, 128), BF16),
            pltpu.VMEM((2, 128, 128), F32),
            pltpu.VMEM((2, 2, 64, 128), BF16),
            pltpu.VMEM((2, 2, 64, 128), F32),
            pltpu.VMEM((8, 8, 64, 128), BF16),
            pltpu.VMEM((5, 8, 2, 16, 128), BF16),
            pltpu.VMEM((1, 128, 128), F32),
            pltpu.VMEM((1, 128, 128), F32),
            pltpu.VMEM((2, 128, 128), F32),
            pltpu.VMEM((4, 8, 128), F32),
            pltpu.VMEM((5, 48, 128), F32),
            pltpu.VMEM((128, 128), F32),
            pltpu.VMEM((len(LINES), 64, 128), F32),
            pltpu.VMEM((len(ROWS2D), 80, 128), F32),
            pltpu.VMEM((len(ROWS2D), 80, 128), F32),
            pltpu.VMEM((5, 80, 128), F32),
            pltpu.VMEM((COUNT * 64, 256), BF16),
            pltpu.VMEM((COUNT * 64, 512), F32),
            pltpu.VMEM((len(LINES), 80, 128), F32),
            dma, dma, dma((4,)), dma((4,)), dma((12,)), dma((12,)), dma((16,)), dma((16,)),
            dma, dma, dma, dma, dma((3,)), dma((3,)), dma((8,)),
        ],
        compiler_params=pltpu.CompilerParams(
            collective_id=0, has_side_effects=True, vmem_limit_bytes=58 * 1024 * 1024),
    )(potentials, orbitals, energies.reshape(1, 32), local_potential, inverse_factor)


def solution(mesh):
    in_specs = (P("pot", "grid", None), P(None, "grid", "pot"), P(), P(), P())
    out_specs = (P("pot", "grid", None), P("pot", None))
    return jax.shard_map(local, mesh=mesh, in_specs=in_specs, out_specs=out_specs, check_vma=False)
```

```python
import jax
import jax.numpy as jnp
from jax import lax
from jax.experimental import pallas as pl
from jax.experimental.pallas import tpu as pltpu
from jax.sharding import PartitionSpec as P

MESH = pl.DeviceIdType.MESH
F32 = jnp.float32
BF16 = jnp.bfloat16
NZ = 32
NPAIR = 32
ROWS2D = [(dz, dy) for dz in range(-3, 4) for dy in range(-3, 4) if abs(dz) + abs(dy) <= 3]
INDEX2D = {pair: number for number, pair in enumerate(ROWS2D)}
OFFSETS = [
    (dz, dy, dx)
    for dz, dy in ROWS2D
    for dx in range(-3, 4)
    if abs(dz) + abs(dy) + abs(dx) <= 3
]
COUNT = len(OFFSETS)
LINES = sorted({(3 + zl + dz, 3 + yl + dy) for dz, dy in ROWS2D for zl in range(2) for yl in range(2)})
LINE_INDEX = {line: number for number, line in enumerate(LINES)}
CROSS = [(0, 0), (1, 0), (-1, 0), (0, 1), (0, -1)]
FAR = 1e30


def tile_of(p):
    core, x, y, low = p % 2, (p // 2) % 4, (p // 8) % 8, p // 64
    return low * 2 + core, y * 4 + x + (y % 2) * (3 - 2 * x)


def device_of(zp, yt):
    y, s = yt // 4, yt % 4
    return (zp // 2) * 64 + y * 8 + (s + (y % 2) * (3 - 2 * s)) * 2 + zp % 2


def place(zt, yt):
    return device_of(zt % 4, yt), zt // 4


def line_sets(dz, dy):
    return [(3 + zl + dz, 3 + yl + dy) for zl in range(2) for yl in range(2)]


def pack_helpers():
    n = lax.broadcasted_iota(jnp.int32, (512, 256), 0)
    k = lax.broadcasted_iota(jnp.int32, (512, 256), 1)
    want = (n % 32) * 8 + (n // 128) * 2 + (n // 32) % 2
    choose = jnp.where(k == want, 1.0, 0.0).astype(BF16)
    fold = lax.broadcasted_iota(jnp.int32, (16, 32), 1) % 16 == lax.broadcasted_iota(jnp.int32, (16, 32), 0)
    return choose, jnp.where(fold, 1.0, 0.0).astype(BF16)


def pack_orbitals(orb, choose, fold, packed):
    flat = orb[...].astype(F32).reshape(256, 32).astype(BF16)
    lanes = jnp.dot(choose, flat, preferred_element_type=F32)
    row = lax.broadcasted_iota(jnp.int32, (512, 32), 0)
    cell = lax.broadcasted_iota(jnp.int32, (512, 32), 1)
    lanes = jnp.where(cell // 16 == (row // 64) % 2, lanes, 0.0).astype(BF16)
    folded = lax.dot_general(fold, lanes, (((1,), (1,)), ((), ())), preferred_element_type=F32)
    for pair in range(4):
        packed[pair] = folded[:, pair * 128 : pair * 128 + 128].astype(BF16)


def build_weights(zt, yt, columns, energies, pads, ls, bl, wf, sf):
    for m in range(5):
        pp = yt - 2 + m
        ok = jnp.logical_and(pp >= 0, pp < NPAIR)
        pads[m, 0:8, :] = jnp.full((8, 128), FAR, F32)
        pads[m, 40:48, :] = jnp.full((8, 128), FAR, F32)
        pads[m, 8:40, :] = jnp.where(ok, columns[m], FAR)
        ls[m * 8 : m * 8 + 8, :] = pads[m, pl.ds(2 * zt + 5, 8), :]
    lt = ls[...].T
    for number, (k, r) in enumerate(LINES):
        m, yl = (r + 1) // 2, (r + 1) % 2
        c = m * 8 + k
        bl[number] = jnp.broadcast_to(lt[yl * 64 : yl * 64 + 64, c : c + 1], (64, 128))
    group = lax.broadcasted_iota(jnp.int32, (64, 128), 1) // 32
    row = energies[...]
    shift3 = 3.0 - jnp.concatenate([row, row, row, row], axis=1)
    zeros = jnp.zeros((8, 128), F32)
    for number, (dz, dy) in enumerate(ROWS2D):
        at = None
        for l, line in enumerate(line_sets(dz, dy)):
            here = bl[LINE_INDEX[line]]
            at = here if at is None else jnp.where(group == l, here, at)
        wf[number, 0:8, :] = zeros
        wf[number, 72:80, :] = zeros
        wf[number, 8:72, :] = jnp.where(at > 0.1 * FAR, 0.0, 0.4 / (at + shift3))
    for number, (dz, dy) in enumerate(CROSS):
        i = INDEX2D[(dz, dy)]
        total = wf[i, 3:75, :] + wf[i, 5:77, :]
        for ez, ey in CROSS[1:]:
            total = total + wf[INDEX2D[(dz + ez, dy + ey)], 4:76, :]
        sf[number, 4:76, :] = total


def build_orbitals(orbs, wf, pf):
    group = lax.broadcasted_iota(jnp.int32, (16, 128), 1) // 32
    zeros = jnp.zeros((8, 128), F32)
    for number, (dz, dy) in enumerate(ROWS2D):
        pf[number, 0:8, :] = zeros
        pf[number, 72:80, :] = zeros
        for h in range(2):
            for xq in range(2):
                orb = None
                for l, (k, r) in enumerate(line_sets(dz, dy)):
                    q, zl = (k + 1) // 2, (k + 1) % 2
                    unit = orbs[q, r, h].astype(F32)
                    shift = (l * 32 - xq * 64 - zl * 32) % 128
                    if shift:
                        unit = pltpu.roll(unit, shift, 1)
                    orb = unit if orb is None else jnp.where(group == l, unit, orb)
                x0 = 8 + h * 32 + xq * 16
                pf[number, x0 : x0 + 16, :] = orb * wf[number, x0 : x0 + 16, :]


def build_products(wf, pf, sf, qb):
    def w(dz, dy, dx):
        return wf[INDEX2D[(dz, dy)], 8 + dx : 72 + dx, :]

    def s1(dz, dy, dx):
        return sf[CROSS.index((dz, dy)), 8 + dx : 72 + dx, :]

    def unit(axis, sign):
        return tuple(sign if a == axis else 0 for a in range(3))

    def plus(a, b):
        return tuple(x + y for x, y in zip(a, b))

    mine = -0.25 * pf[INDEX2D[(0, 0)], 8:72, :]
    for number, offset in enumerate(OFFSETS):
        dist = sum(abs(c) for c in offset)
        steps = []
        for axis in range(3):
            if offset[axis]:
                steps.append((unit(axis, 1 if offset[axis] > 0 else -1), abs(offset[axis])))
        if dist == 0:
            orb = 1.248 / w(0, 0, 0)
            path = orb + 1.6 * s1(0, 0, 0)
        elif dist == 1:
            e = offset
            w0, we = w(0, 0, 0), w(*e)
            path = 1.52 + w0 * (s1(0, 0, 0) - we) + we * s1(*e)
            for axis in range(3):
                if not e[axis]:
                    for sign in (1, -1):
                        b = unit(axis, sign)
                        path = path + w(*b) * w(*plus(b, e))
        elif dist == 2:
            if len(steps) == 1:
                path = 1.6 * w(*steps[0][0])
            else:
                path = 1.6 * (w(*steps[0][0]) + w(*steps[1][0]))
        elif len(steps) == 1:
            a = steps[0][0]
            path = w(*a) * w(*plus(a, a))
        elif len(steps) == 2:
            (a, b) = (steps[0][0], steps[1][0]) if steps[0][1] == 2 else (steps[1][0], steps[0][0])
            ab = w(*plus(a, b))
            path = w(*a) * (w(*plus(a, a)) + ab) + w(*b) * ab
        else:
            a, b, c = (s[0] for s in steps)
            ab, ac, bc = w(*plus(a, b)), w(*plus(a, c)), w(*plus(b, c))
            path = w(*a) * (ab + ac) + w(*b) * (ab + bc) + w(*c) * (ac + bc)
        dz, dy, dx = offset
        q = mine * pf[INDEX2D[(dz, dy)], 8 + dx : 72 + dx, :] * path
        high = q.astype(BF16)
        qb[number * 64 : number * 64 + 64, 0:128] = high
        qb[number * 64 : number * 64 + 64, 128:256] = (q - high.astype(F32)).astype(BF16)


def build_coefficients(qb, coef):
    k = lax.broadcasted_iota(jnp.int32, (256, 512), 0)
    n = lax.broadcasted_iota(jnp.int32, (256, 512), 1)
    spread = jnp.where((k % 128) // 32 == n // 128, 1.0, 0.0).astype(BF16)

    @pl.loop(0, 9)
    def _(step):
        rows = pl.ds(pl.multiple_of(step * 448, 448), 448)
        coef[rows, :] = jnp.dot(qb[rows, :], spread, preferred_element_type=F32)


def place_lines(source, inside, vf):
    zeros = jnp.zeros((8, 128), F32)
    for number, (k, r) in enumerate(LINES):
        here = 3 <= k <= 4 and 3 <= r <= 4
        if here != inside:
            continue
        vf[number, 0:8, :] = zeros
        vf[number, 72:80, :] = zeros
        vf[number, 8:72, :] = source[k - 3, r - 3] if here else source[k, r].astype(F32)


def apply_stencil(vf, coef, inside, start):
    trial = []
    for l in range(4):
        zl, yl = l // 2, l % 2
        total = start[l]
        for number, (dz, dy, dx) in enumerate(OFFSETS):
            line = (3 + zl + dz, 3 + yl + dy)
            if (3 <= line[0] <= 4 and 3 <= line[1] <= 4) != inside:
                continue
            field = vf[LINE_INDEX[line], 8 + dx : 72 + dx, :]
            total = total + coef[number * 64 : number * 64 + 64, l * 128 : l * 128 + 128] * field
        trial.append(total)
    return trial


def pots_by_cells(trial):
    columns = []
    for zl in range(2):
        plane = jnp.concatenate([trial[2 * zl], trial[2 * zl + 1]], axis=0)
        columns.append(plane.T.astype(BF16))
    return columns


def gram_part(columns):
    gram = None
    for part in columns:
        part = lax.dot_general(part, part, (((1,), (1,)), ((), ())), preferred_element_type=F32)
        gram = part if gram is None else gram + part
    return gram * (1.0 / 131072.0)


NEIGHBOURS = [
    (1, 1, 1, 1, 0, 2), (1, -1, 1, 1, 0, 2), (-1, 1, 0, 1, 0, 2), (-1, -1, 0, 1, 0, 2),
    (1, 1, 0, 1, 1, 1), (1, -1, 0, 1, 0, 1), (-1, 1, 1, 1, 1, 1), (-1, -1, 1, 1, 0, 1),
    (0, 2, 0, 2, 1, 1), (0, -2, 0, 2, 0, 1), (2, 0, 1, 1, 0, 2), (-2, 0, 0, 1, 0, 2),
    (0, 1, 0, 2, 0, 2), (0, -1, 0, 2, 0, 2), (1, 0, 0, 2, 0, 2), (-1, 0, 0, 2, 0, 2),
]
ORB_NEIGHBOURS = [
    (1, 0, 0, 2), (-1, 0, 0, 2), (0, 1, 0, 2), (0, -1, 0, 2), (2, 0, 0, 2), (-2, 0, 0, 2),
    (1, 1, 0, 2), (1, -1, 0, 2), (-1, 1, 0, 2), (-1, -1, 0, 2), (0, 2, 1, 1), (0, -2, 0, 1),
]


def ring(distance, size):
    return min(distance, size - distance)


OTHERS = sorted(
    ((y, x, z, c) for y in range(8) for x in range(4) for z in range(2) for c in range(2) if y or x or z or c),
    key=lambda d: (-(ring(d[0], 8) + ring(d[1], 4) + d[2]), d),
)


def kernel(pot_far, orb_far, energies_far, loc_far, factor_far, out, margins,
           orb, energies, columns, factor, orb_in, recv, lines, own, halo, orbs, gram, gram_back, ug, parts, pads, ls, bl, wf, pf, sf, qb, coef, vf,
           row_send, row_recv, move_send, move_recv, orb_send, orb_recv, halo_send, halo_recv,
           gram_send, gram_recv, back_send, back_recv, part_send, part_recv, load_sem):
    me, g = lax.axis_index("pot"), lax.axis_index("grid")
    zp, yt = tile_of(me)
    zt = g * 4 + zp
    ys = [(me // 8 + d) % 8 * 8 for d in range(8)]
    xs = [(me // 2 + d) % 4 * 2 for d in range(4)]
    zs = [me // 64 * 64, (1 - me // 64) * 64]
    cs = [me % 2, 1 - me % 2]

    def others():
        for y, x, z, c in OTHERS:
            yield ys[y] + xs[x] + zs[z] + cs[c]

    def cells_of(y, x, z, c):
        across = ys[y] // 8 % 2
        to_yt = ys[y] // 2 + xs[x] // 2 + across * (3 - xs[x])
        to_plane = zs[z] // 16 + cs[c] * 2
        return pot_far.at[0, pl.ds(to_plane, 2), pl.ds(pl.multiple_of(to_yt * 128, 128), 128)]

    def near(a, b):
        return place((zt + a + 16) % 16, (yt + b + 32) % 32)

    loads = [
        pltpu.make_async_copy(orb_far, orb, load_sem.at[0]),
        pltpu.make_async_copy(energies_far, energies, load_sem.at[1]),
        pltpu.make_async_copy(factor_far, factor, load_sem.at[2]),
    ]
    for m in range(5):
        at = pl.multiple_of(jnp.clip(yt - 2 + m, 0, NPAIR - 1) * 128, 128)
        loads.append(pltpu.make_async_copy(loc_far.at[:, pl.ds(at, 128)], columns.at[m], load_sem.at[3 + m]))
    for load in loads:
        load.start()

    barrier = pltpu.get_barrier_semaphore()
    for to in others():
        pl.semaphore_signal(barrier, inc=1, device_id=(to, g), device_id_type=MESH)
    for step in range(1, 4):
        pl.semaphore_signal(barrier, inc=1, device_id=(me, (g + step) % 4), device_id_type=MESH)
    for a, b, *_ in ORB_NEIGHBOURS:
        pl.semaphore_signal(barrier, inc=1, device_id=near(a, b), device_id_type=MESH)

    choose, fold = pack_helpers()
    loads[0].wait()
    pack_orbitals(orb, choose, fold, orb_in)
    pl.semaphore_wait(barrier, len(OTHERS) + 3 + len(ORB_NEIGHBOURS))

    row, half = me // 2, me % 2
    low, landing = row % 2, (row % 2) * 2 + half
    moves = []
    for to_zp in range(4):
        to = device_of(to_zp, row // 2)
        target = orbs.at[2, 3 + low, half]
        move = pltpu.make_async_remote_copy(
            orb_in.at[to_zp], target, move_send.at[to_zp], move_recv.at[landing],
            device_id=(to, g), device_id_type=MESH)
        moves.append((to, move))
        pl.when(to != me)(move.start)
        pl.when(to == me)(pltpu.make_async_copy(orb_in.at[to_zp], target, move_recv.at[landing]).start)

    for to, offsets in zip(others(), OTHERS):
        pltpu.make_async_remote_copy(
            cells_of(*offsets), recv.at[:, me, :], row_send, row_recv,
            device_id=(to, g), device_id_type=MESH).start()
    pltpu.make_async_copy(cells_of(0, 0, 0, 0), recv.at[:, me, :], row_recv).start()

    for yl in range(2):
        for h in range(2):
            landed = orbs.at[2, 3 + yl, h]
            pltpu.make_async_copy(landed, landed, move_recv.at[yl * 2 + h]).wait()
    orb_copies = []
    for number, (a, b, y0, ny) in enumerate(ORB_NEIGHBOURS):
        yy = 3 - 2 * b + y0
        orb_copies.append(pltpu.make_async_remote_copy(
            orbs.at[2, 3 + y0 : 3 + y0 + ny], orbs.at[2 - a, yy : yy + ny],
            orb_send.at[number], orb_recv.at[number], device_id=near(a, b), device_id_type=MESH))
        orb_copies[-1].start()

    pltpu.make_async_copy(recv, recv, row_recv).wait()
    for zl in range(2):
        plane = recv[zl].T
        for yl in range(2):
            line = plane[yl * 64 : yl * 64 + 64]
            own[zl, yl] = line
            lines[zl, yl] = line.astype(BF16)
    copies = []
    for number, (a, b, z0, nz, y0, ny) in enumerate(NEIGHBOURS):
        zz, yy = 3 - 2 * a + z0, 3 - 2 * b + y0
        copies.append(pltpu.make_async_remote_copy(
            lines.at[z0 : z0 + nz, y0 : y0 + ny], halo.at[zz : zz + nz, yy : yy + ny],
            halo_send.at[number], halo_recv.at[number], device_id=near(a, b), device_id_type=MESH))
        copies[-1].start()

    for load in loads[1:]:
        load.wait()
    build_weights(zt, yt, columns, energies, pads, ls, bl, wf, sf)

    for copy in orb_copies:
        copy.wait_recv()
    build_orbitals(orbs, wf, pf)
    build_products(wf, pf, sf, qb)
    build_coefficients(qb, coef)
    place_lines(own, True, vf)
    partial = apply_stencil(vf, coef, True, [own[l // 2, l % 2] for l in range(4)])
    for copy in copies:
        copy.wait_recv()
    place_lines(halo, False, vf)
    columns = pots_by_cells(apply_stencil(vf, coef, False, partial))

    gram[0] = gram_part(columns)
    for to in others():
        pltpu.make_async_remote_copy(
            gram.at[:, to, :], gram_back.at[:, me, :], gram_send, gram_recv,
            device_id=(to, g), device_id_type=MESH).start()
    pltpu.make_async_copy(gram.at[:, me, :], gram_back.at[:, me, :], gram_recv).start()
    for zl in range(2):
        ug[zl] = jnp.dot(factor[...], columns[zl], preferred_element_type=F32)
    cells = out.at[0, pl.ds(zp * 2, 2), pl.ds(pl.multiple_of(yt * 128, 128), 128)]
    for to in others():
        pltpu.make_async_remote_copy(
            ug.at[:, to, :], cells, back_send, back_recv, device_id=(to, g), device_id_type=MESH).start()
    pltpu.make_async_copy(ug.at[:, me, :], cells, back_recv).start()

    pltpu.make_async_copy(gram_back, gram_back, gram_recv).wait()
    parts[0] = jnp.broadcast_to(jnp.sum(gram_back[0], axis=0, keepdims=True), (8, 128))
    part_copies = []
    for step in range(1, 4):
        part_copies.append(pltpu.make_async_remote_copy(
            parts.at[0], parts.at[4 - step], part_send.at[step - 1], part_recv.at[step - 1],
            device_id=(me, (g + step) % 4), device_id_type=MESH))
        part_copies[-1].start()
    for copy in orb_copies + copies:
        copy.wait_send()
    for to, move in moves:
        pl.when(to != me)(move.wait_send)
    pltpu.make_async_copy(recv.at[:, 0:127, :], recv.at[:, 0:127, :], row_send).wait()

    for copy in part_copies:
        copy.wait()
    total = None
    for slab in range(4):
        part = parts[(slab - g + 4) % 4]
        total = part if total is None else total + part
    margins[...] = total[0:1]
    pltpu.make_async_copy(out, out, back_recv).wait()
    pltpu.make_async_copy(ug.at[:, 0:127, :], ug.at[:, 0:127, :], back_send).wait()
    pltpu.make_async_copy(gram.at[:, 0:127, :], gram.at[:, 0:127, :], gram_send).wait()


def local(potentials, orbitals, energies, local_potential, inverse_factor):
    hbm = pl.BlockSpec(memory_space=pltpu.HBM)
    vmem = pl.BlockSpec(memory_space=pltpu.VMEM)
    dma = pltpu.SemaphoreType.DMA
    return pl.pallas_call(
        kernel,
        out_shape=(jax.ShapeDtypeStruct((1, 8, 4096), F32), jax.ShapeDtypeStruct((1, 128), F32)),
        in_specs=[hbm] * 5,
        out_specs=(hbm, vmem),
        scratch_shapes=[
            pltpu.VMEM((32, 8, 32), BF16),
            pltpu.VMEM((1, 32), F32),
            pltpu.VMEM((5, 32, 128), F32),
            pltpu.VMEM((128, 128), BF16),
            pltpu.VMEM((4, 16, 128), BF16),
            pltpu.VMEM((2, 128, 128), F32),
            pltpu.VMEM((2, 2, 64, 128), BF16),
            pltpu.VMEM((2, 2, 64, 128), F32),
            pltpu.VMEM((8, 8, 64, 128), BF16),
            pltpu.VMEM((5, 8, 2, 16, 128), BF16),
            pltpu.VMEM((1, 128, 128), F32),
            pltpu.VMEM((1, 128, 128), F32),
            pltpu.VMEM((2, 128, 128), F32),
            pltpu.VMEM((4, 8, 128), F32),
            pltpu.VMEM((5, 48, 128), F32),
            pltpu.VMEM((128, 128), F32),
            pltpu.VMEM((len(LINES), 64, 128), F32),
            pltpu.VMEM((len(ROWS2D), 80, 128), F32),
            pltpu.VMEM((len(ROWS2D), 80, 128), F32),
            pltpu.VMEM((5, 80, 128), F32),
            pltpu.VMEM((COUNT * 64, 256), BF16),
            pltpu.VMEM((COUNT * 64, 512), F32),
            pltpu.VMEM((len(LINES), 80, 128), F32),
            dma, dma, dma((4,)), dma((4,)), dma((12,)), dma((12,)), dma((16,)), dma((16,)),
            dma, dma, dma, dma, dma((3,)), dma((3,)), dma((8,)),
        ],
        compiler_params=pltpu.CompilerParams(
            collective_id=0, has_side_effects=True, vmem_limit_bytes=58 * 1024 * 1024),
    )(potentials, orbitals, energies.reshape(1, 32), local_potential, inverse_factor)


def solution(mesh):
    in_specs = (P("pot", "grid", None), P(None, "grid", "pot"), P(), P(), P())
    out_specs = (P("pot", "grid", None), P("pot", None))
    return jax.shard_map(local, mesh=mesh, in_specs=in_specs, out_specs=out_specs, check_vma=False)
```
